32 devices in a mesh: row: 4 (over z), col: 8 (over y, x, core).
Axes of the slice: x: 2, y: 2, z: 4, core: 2. Of those that a mesh axis runs over, the one named last changes fastest.
Arguments:
- inverse_first: float32 [512, 512], P('row'), may hold values from -0.4 to 2
- inverse_second: float32 [512, 512], P('row'), may hold values from -0.4 to 2
- coupling: float32 [512, 512], P('row'), may hold values from -0.25 to 0.25
- panel_first: float32 [16384, 512], P('row', 'col'), may hold values from -0.1875 to 0.1875
- panel_second: float32 [16384, 512], P('row', 'col'), may hold values from -0.1875 to 0.1875
- rhs_first: float32 [512, 2048], P('row', 'col'), may hold values from -6 to 6
- rhs_second: float32 [512, 2048], P('row', 'col'), may hold values from -6 to 6
- rhs_rest: float32 [16384, 2048], P('row', 'col'), may hold values from -6 to 6
Outputs:
- solved_first: float32 [512, 2048], P('row', 'col')
- solved_second: float32 [512, 2048], P('row', 'col')
- updated: float32 [16384, 2048], P('row', 'col')
The draws below stay inside these ranges and needn't reach their ends.
All inputs are finite; a program needn't handle non-finite values.
Results may differ from the reference program's by a relative error of at most 0.00011.
Values sent between devices are 32-bit elements; how exact they have to be, the bound alone decides.
No kernel may reach another device: no remote copies, remote signals or barrier semaphores. Data moves between devices by JAX's collectives and lax.ppermute only.
A program may use at most 64 MiB of HBM per device.

```python
import math
import jax
import jax.numpy as jnp
from jax import lax

NB = 512
SAMPLES = 2048
REST = 16384


def lower_factor(key):
    key_off, key_diag = jax.random.split(key)
    rows = lax.broadcasted_iota(jnp.int32, (NB, NB), 0)
    cols = lax.broadcasted_iota(jnp.int32, (NB, NB), 1)
    offdiag = jnp.clip(jax.random.normal(key_off, (NB, NB), jnp.float32), -4.0, 4.0) * (0.6 / math.sqrt(NB))
    diag_vals = jax.random.uniform(key_diag, (NB,), jnp.float32, 0.7, 1.4)
    diag_full = jnp.broadcast_to(diag_vals[:, None], (NB, NB))
    zeros_full = jnp.zeros((NB, NB), jnp.float32)
    return jnp.where(rows > cols, offdiag, jnp.where(rows == cols, diag_full, zeros_full))


def draw_inverse_first(key, part):
    return lower_factor(jax.random.fold_in(key, 11))


def draw_inverse_second(key, part):
    return lower_factor(jax.random.fold_in(key, 23))


def block_levels(own_key, shape, shards, low, top_value):
    loudness = 1.0
    for position, parts in shards:
        steps = jax.random.uniform(jax.random.fold_in(jax.random.fold_in(own_key, 6), position), (parts,), jnp.float32, low / len(shards), top_value / len(shards))
        loudness = loudness * jnp.repeat(jnp.exp(steps), shape[position] // parts).reshape((-1,) + (1,) * (len(shape) - 1 - position))
    return loudness


def scatter_about(rng, extent, scale, most, cuts=(), kind=jnp.bfloat16):
    drawn = scale * jax.random.normal(rng, extent, jnp.float32)
    if cuts:
        drawn = drawn * block_levels(rng, extent, cuts, -0.22, 0.18)
    return jnp.clip(drawn, -most, most).astype(kind)


def setup_inputs(seed: int = 0) -> dict:
    keys = jax.random.split(jax.random.key(seed), 9)
    inverse_first = draw_inverse_first(jax.random.fold_in(keys[8], 71), 0)
    inverse_second = draw_inverse_second(jax.random.fold_in(keys[8], 71), 0)
    coupling = scatter_about(keys[2], (NB, NB), NB ** -0.5, 0.25, ((0, 4),), jnp.float32)
    panel_first = scatter_about(keys[3], (REST, NB), (2 * NB) ** -0.5, 0.1875, ((0, 4), (1, 8)), jnp.float32)
    panel_second = scatter_about(keys[4], (REST, NB), (2 * NB) ** -0.5, 0.1875, ((0, 4), (1, 8)), jnp.float32)
    rhs_first = scatter_about(keys[5], (NB, SAMPLES), 1.0, 6.0, ((0, 4), (1, 8)), jnp.float32)
    rhs_second = scatter_about(keys[6], (NB, SAMPLES), 1.0, 6.0, ((0, 4), (1, 8)), jnp.float32)
    rhs_rest = scatter_about(keys[7], (REST, SAMPLES), 1.0, 6.0, ((0, 4), (1, 8)), jnp.float32)
    return dict(inverse_first=inverse_first, inverse_second=inverse_second, coupling=coupling, panel_first=panel_first, panel_second=panel_second, rhs_first=rhs_first, rhs_second=rhs_second, rhs_rest=rhs_rest)


def product(left, right):
    return jnp.dot(left, right, precision=lax.Precision.HIGHEST, preferred_element_type=jnp.float32)


def reference(inverse_first, inverse_second, coupling, panel_first, panel_second, rhs_first, rhs_second, rhs_rest):
    solved_first = product(inverse_first, rhs_first)
    reduced = rhs_second - product(coupling, solved_first)
    solved_second = product(inverse_second, reduced)
    updated = rhs_rest - product(panel_first, solved_first) - product(panel_second, solved_second)
    return solved_first, solved_second, updated
```

```python
import functools

import jax
import jax.numpy as jnp
from jax import lax
from jax.experimental import pallas as pl
from jax.experimental.pallas import tpu as pltpu
from jax.sharding import PartitionSpec as P

VMEM_BYTES = 24 * 2**20
INNER = 8
CORE, ACROSS, UP = 1, 2, 4
FIRST, SECOND = 0, 1
GROUPS = (
    (
        (FIRST, 0), (FIRST, CORE), (SECOND, 0), (SECOND, CORE),
        (FIRST, UP), (FIRST, UP | CORE), (SECOND, ACROSS), (SECOND, ACROSS | CORE),
    ),
    ((FIRST, ACROSS), (FIRST, ACROSS | CORE), (SECOND, UP), (SECOND, UP | CORE)),
    (
        (FIRST, ACROSS | UP), (FIRST, ACROSS | UP | CORE),
        (SECOND, ACROSS | UP), (SECOND, ACROSS | UP | CORE),
    ),
)


def split(value):
    high = value.astype(jnp.bfloat16)
    return high, (value - high.astype(jnp.float32)).astype(jnp.bfloat16)


def product(left, right, contract=1):
    def one(a, b):
        return lax.dot_general(
            a, b, (((contract,), (0,)), ((), ())), preferred_element_type=jnp.float32
        )

    return one(left[0], right[0]) + one(left[0], right[1]) + one(left[1], right[0])


def pack_kernel(*refs):
    (*matrices, first, second), out = refs[:-1], refs[-1]
    rows, width = first.shape
    even = lax.rem(lax.axis_index("col"), 2) == 0
    for k, ref in enumerate(matrices):
        out[k * rows : (k + 1) * rows, :] = jnp.where(even, ref[:, :width], ref[:, width:])
    out[3 * rows : 4 * rows, :] = first[...]
    out[4 * rows :, :] = second[...]


def pack_rows(own):
    rows, width = own[3].shape
    whole = pl.BlockSpec(memory_space=pltpu.VMEM)
    return pl.pallas_call(
        pack_kernel,
        out_shape=jax.ShapeDtypeStruct((5 * rows, width), jnp.float32),
        in_specs=[whole] * 5,
        out_specs=whole,
        cost_estimate=pl.CostEstimate(flops=0, bytes_accessed=0, transcendentals=0),
    )(*own)


def solve_kernel(steps, block, *refs):
    own, refs = refs[:5], refs[5:]
    pieces, (others, *refs) = refs[: steps - 1], refs[steps - 1 :]
    outs, (first_out, second_out, *scratch) = refs[: 2 * len(GROUPS)], refs[2 * len(GROUPS) :]
    matrices, right_first, right_second, solved = scratch
    here = lax.axis_index("row")
    lane = lax.axis_index("col")
    even = lax.rem(lane, 2) == 0
    rows, width = own[3].shape[0], matrices.shape[2] // 2

    def at(step):
        return pl.ds(pl.multiple_of(lax.rem(here + steps - step, steps) * rows, rows), rows)

    for k in range(3):
        matrices[k, at(0), :] = own[k][...]
    right_first[at(0), :] = own[3][...]
    right_second[at(0), :] = own[4][...]
    for j, piece in enumerate(pieces):
        right_first[at(j + 1), :] = piece[3 * rows : 4 * rows, :]
        right_second[at(j + 1), :] = piece[4 * rows :, :]
        for k in range(3):
            mine = piece[k * rows : (k + 1) * rows, :]
            other = others[(3 * j + k) * rows : (3 * j + k + 1) * rows, :]
            matrices[k, at(j + 1), :width] = jnp.where(even, mine, other)
            matrices[k, at(j + 1), width:] = jnp.where(even, other, mine)
    solved[0] = product(split(matrices[0]), split(right_first[...]))
    reduced = right_second[...] - product(split(matrices[2]), split(solved[0]))
    solved[1] = product(split(matrices[1]), split(reduced))
    first_out[...] = solved[0, at(0), :]
    second_out[...] = solved[1, at(0), :]

    inner = lax.rem(lane, INNER)
    outer = solved.shape[1] // (INNER * block)
    for group, (high_out, low_out) in zip(GROUPS, zip(outs[::2], outs[1::2])):
        to = 0
        for part, m in group:
            which = lax.bitwise_xor(inner, m)
            for o in range(outer):
                start = pl.multiple_of((o * INNER + which) * block, block)
                high, low = split(solved[part, pl.ds(start, block), :])
                high_out[to : to + block, :] = high
                low_out[to : to + block, :] = low
                to += block


def solve(steps, block, own, pieces, others):
    rows, width = own[3].shape
    depth = rows * steps
    outs = [
        jax.ShapeDtypeStruct((len(group) * depth // INNER, width), jnp.bfloat16)
        for group in GROUPS
        for _ in range(2)
    ]
    outs += [jax.ShapeDtypeStruct((rows, width), jnp.float32)] * 2
    whole = pl.BlockSpec(memory_space=pltpu.VMEM)
    operands = [*own, *pieces, others]
    return pl.pallas_call(
        functools.partial(solve_kernel, steps, block),
        out_shape=outs,
        in_specs=[whole] * len(operands),
        out_specs=[whole] * len(outs),
        scratch_shapes=[
            pltpu.VMEM((3, depth, depth), jnp.float32),
            pltpu.VMEM((depth, width), jnp.float32),
            pltpu.VMEM((depth, width), jnp.float32),
            pltpu.VMEM((2, depth, width), jnp.float32),
        ],
        compiler_params=pltpu.CompilerParams(vmem_limit_bytes=VMEM_BYTES),
        cost_estimate=pl.CostEstimate(flops=0, bytes_accessed=0, transcendentals=0),
    )(*operands)


def turn_kernel(count, *refs):
    panels, (high, low) = refs[:count], refs[count:]
    high[...], low[...] = split(jnp.concatenate([ref[...] for ref in panels], axis=0).T)


def turn(panels):
    rows, depth = panels[0].shape[1], sum(p.shape[0] for p in panels)
    tile = min(rows, 1024)
    return pl.pallas_call(
        functools.partial(turn_kernel, len(panels)),
        grid=(rows // tile,),
        out_shape=[jax.ShapeDtypeStruct((rows, depth), jnp.bfloat16)] * 2,
        in_specs=[pl.BlockSpec((p.shape[0], tile), lambda i: (0, i)) for p in panels],
        out_specs=[pl.BlockSpec((tile, depth), lambda i: (i, 0))] * 2,
        compiler_params=pltpu.CompilerParams(vmem_limit_bytes=VMEM_BYTES),
        cost_estimate=pl.CostEstimate(flops=0, bytes_accessed=0, transcendentals=0),
    )(*panels)


def update_kernel(count, *refs):
    before, after = refs[4 * count :]
    total = before[...]
    for j in range(count):
        a, b, c, d = (ref[...] for ref in refs[4 * j : 4 * j + 4])
        total = total - product((a, b), (c, d))
    after[...] = total


def update(pairs, before, in_place=False):
    rows, width = pairs[0][0][0].shape[0], before.shape[1]
    tile = min(rows, 512)
    panel = [pl.BlockSpec((tile, left[0].shape[1]), lambda i: (i, 0)) for left, _ in pairs]
    factor = [pl.BlockSpec(right[0].shape, lambda i: (0, 0)) for _, right in pairs]
    depth = sum(left[0].shape[1] for left, _ in pairs)
    return pl.pallas_call(
        functools.partial(update_kernel, len(pairs)),
        grid=(rows // tile,),
        out_shape=jax.ShapeDtypeStruct(before.shape, jnp.float32),
        in_specs=[x for p, f in zip(panel, factor) for x in (p, p, f, f)]
        + [pl.BlockSpec((tile, width), lambda i: (i, 0))],
        out_specs=pl.BlockSpec((tile, width), lambda i: (i, 0)),
        input_output_aliases={4 * len(pairs): 0} if in_place else {},
        compiler_params=pltpu.CompilerParams(vmem_limit_bytes=VMEM_BYTES),
        cost_estimate=pl.CostEstimate(flops=0, bytes_accessed=0, transcendentals=0),
    )(*[x for left, right in pairs for x in (*left, *right)], before)


def finish_kernel(count, *refs):
    panels, (high, low, before, after) = refs[:count], refs[count:]
    panel = jnp.concatenate([ref[...] for ref in panels], axis=0)
    after[...] = before[...] - product(split(panel), (high[...], low[...]), contract=0)


def finish(panels, factor, before, start):
    count, rows, depth = len(panels), panels[0].shape[1], sum(p.shape[0] for p in panels)
    width = before.shape[1]
    tile = min(rows, 512)
    first = start // tile
    return pl.pallas_call(
        functools.partial(finish_kernel, count),
        grid=(rows // tile,),
        out_shape=jax.ShapeDtypeStruct(before.shape, jnp.float32),
        in_specs=[pl.BlockSpec((p.shape[0], tile), lambda i: (0, i)) for p in panels]
        + [pl.BlockSpec(f.shape, lambda i: (0, 0)) for f in factor]
        + [pl.BlockSpec((tile, width), lambda i: (i + first, 0))],
        out_specs=pl.BlockSpec((tile, width), lambda i: (i + first, 0)),
        input_output_aliases={count + 2: 0},
        compiler_params=pltpu.CompilerParams(vmem_limit_bytes=VMEM_BYTES),
        cost_estimate=pl.CostEstimate(flops=0, bytes_accessed=0, transcendentals=0),
    )(*panels, *factor, before)


def solution(mesh):
    row_count, col_count = mesh.shape["row"], mesh.shape["col"]

    def swap(value, bit):
        return lax.ppermute(value, "col", [(i, i ^ bit) for i in range(col_count)])

    def shift(value, by):
        return lax.ppermute(value, "row", [(i, (i + by) % row_count) for i in range(row_count)])

    def per_device(
        inverse_first, inverse_second, coupling, panel_first, panel_second,
        rhs_first, rhs_second, rhs_rest,
    ):
        first, second = panel_first.T, panel_second.T
        block = first.shape[0]
        if col_count > INNER:
            groups = [list(range(i, col_count, INNER)) for i in range(INNER)]
            first, second = (
                lax.all_gather(p, "col", axis=0, tiled=True, axis_index_groups=groups)
                for p in (first, second)
            )
        rest = first.shape[1]

        own = (inverse_first, inverse_second, coupling, rhs_first, rhs_second)
        def both(pair, bits=(ACROSS, UP)):
            return tuple(swap(x, bit) for x, bit in zip(pair, bits))

        def beside(pair):
            return both(pair, (CORE, CORE))

        def after(values, *tokens):
            return lax.optimization_barrier((values, tokens))[0]

        near_0 = both((second, first))
        near_1 = both((first, second))
        own_beside = beside((first, second))
        pack = pack_rows(own)
        packs = {1: shift(pack, 1)}
        for j in range(2, row_count // 2 + 1):
            packs[j] = shift(packs[j - 1], 1)
        for j in range(row_count - 1, row_count // 2, -1):
            packs[j] = shift(packs[j + 1] if j < row_count - 1 else after(pack, packs[1]), -1)
        packs = [packs[j] for j in range(1, row_count)]
        beside_0 = beside(after(near_0, own_beside))
        beside_1 = beside(after(near_1, beside_0))
        cuts = [0, 5 * rest // 8, rest]
        far = [
            both(after((near_0[1][:, a:b], near_0[0][:, a:b]), near_1))
            for a, b in zip(cuts[:-1], cuts[1:])
        ]
        turned_0 = turn(
            [first, own_beside[0], second, own_beside[1], near_0[1], beside_0[1], near_0[0], beside_0[0]]
        )
        turned_1 = turn([near_1[0], beside_1[0], near_1[1], beside_1[1]])

        matrix_rows = 3 * rhs_first.shape[0]
        others = swap(jnp.concatenate([p[:matrix_rows] for p in packs], axis=0), CORE)
        *factors, solved_first, solved_second = solve(row_count, block, own, packs, others)
        factors = list(zip(factors[::2], factors[1::2]))
        updated = update([(turned_0, factors[0]), (turned_1, factors[1])], rhs_rest)
        for start, pair in zip(cuts, far):
            pair = after(pair, updated)
            other = beside(pair)
            updated = finish([pair[0], other[0], pair[1], other[1]], factors[2], updated, start)
        return solved_first, solved_second, updated

    in_specs = (P("row", None),) * 3 + (P("row", "col"),) * 5
    return jax.shard_map(
        per_device, mesh=mesh, in_specs=in_specs, out_specs=(P("row", "col"),) * 3, check_vma=False
    )
```

```python
import functools

import jax
import jax.numpy as jnp
from jax import lax
from jax.experimental import pallas as pl
from jax.experimental.pallas import tpu as pltpu
from jax.sharding import PartitionSpec as P

VMEM_BYTES = 24 * 2**20
UPDATE_BYTES = 32 * 2**20
COST = pl.CostEstimate(flops=1024, bytes_accessed=1024, transcendentals=0)
INNER = 8
CORE, ACROSS, UP = 1, 2, 4
FIRST, SECOND = 0, 1
ONE, OTHER = (ACROSS, UP), (UP, ACROSS)


def beyond(masks):
    return masks[1] | CORE, masks[0] | CORE


BOTH = (ACROSS | UP, ACROSS | UP)
GROUPS = tuple(
    tuple((panel, masks) for who in block for masks in (who, beyond(who)) for panel in (FIRST, SECOND))
    for block in (((0, 0), ONE, OTHER), (BOTH,))
)


def split(value):
    high = value.astype(jnp.bfloat16)
    return high, (value - high.astype(jnp.float32)).astype(jnp.bfloat16)


def product(left, right, contract=1):
    def one(a, b):
        return lax.dot_general(
            a, b, (((contract,), (0,)), ((), ())), preferred_element_type=jnp.float32
        )

    return one(left[0], right[0]) + one(left[0], right[1]) + one(left[1], right[0])


def pack_kernel(*refs):
    (*matrices, first, second), out = refs[:-1], refs[-1]
    rows, width = first.shape
    even = lax.rem(lax.axis_index("col"), 2) == 0
    for k, ref in enumerate(matrices):
        out[k * rows : (k + 1) * rows, :] = jnp.where(even, ref[:, :width], ref[:, width:])
    out[3 * rows : 4 * rows, :] = first[...]
    out[4 * rows :, :] = second[...]


def pack_rows(own):
    rows, width = own[3].shape
    whole = pl.BlockSpec(memory_space=pltpu.VMEM)
    return pl.pallas_call(
        pack_kernel,
        out_shape=jax.ShapeDtypeStruct((5 * rows, width), jnp.float32),
        in_specs=[whole] * 5,
        out_specs=whole,
        cost_estimate=COST,
    )(*own)


def solve_kernel(steps, block, *refs):
    own, refs = refs[:5], refs[5:]
    pieces, (early, late, *refs) = refs[: steps - 1], refs[steps - 1 :]
    outs, (first_out, second_out, *scratch) = refs[: 2 * len(GROUPS)], refs[2 * len(GROUPS) :]
    matrices, right_first, right_second, solved = scratch
    here = lax.axis_index("row")
    lane = lax.axis_index("col")
    even = lax.rem(lane, 2) == 0
    rows, width = own[3].shape[0], matrices.shape[2] // 2

    def at(step):
        return pl.ds(pl.multiple_of(lax.rem(here + steps - step, steps) * rows, rows), rows)

    for k in range(3):
        matrices[k, at(0), :] = own[k][...]
    right_first[at(0), :] = own[3][...]
    right_second[at(0), :] = own[4][...]
    for j, piece in enumerate(pieces):
        right_first[at(j + 1), :] = piece[3 * rows : 4 * rows, :]
        right_second[at(j + 1), :] = piece[4 * rows :, :]
        for k in range(3):
            mine = piece[k * rows : (k + 1) * rows, :]
            others, at_row = (late, 3 * (j - 1) + k) if j else (early, k)
            other = others[at_row * rows : (at_row + 1) * rows, :]
            matrices[k, at(j + 1), :width] = jnp.where(even, mine, other)
            matrices[k, at(j + 1), width:] = jnp.where(even, other, mine)
    solved[0] = product(split(matrices[0]), split(right_first[...]))
    reduced = right_second[...] - product(split(matrices[2]), split(solved[0]))
    solved[1] = product(split(matrices[1]), split(reduced))
    first_out[...] = solved[0, at(0), :]
    second_out[...] = solved[1, at(0), :]

    inner = lax.rem(lane, INNER)
    outer = solved.shape[1] // (INNER * block)
    for group, (high_out, low_out) in zip(GROUPS, zip(outs[::2], outs[1::2])):
        to = 0
        for part, (mask, odd_mask) in group:
            which = lax.bitwise_xor(inner, jnp.where(even, mask, odd_mask))
            for o in range(outer):
                start = pl.multiple_of((o * INNER + which) * block, block)
                high, low = split(solved[part, pl.ds(start, block), :])
                high_out[to : to + block, :] = high
                low_out[to : to + block, :] = low
                to += block


def solve(steps, block, own, pieces, others):
    rows, width = own[3].shape
    depth = rows * steps
    outs = [
        jax.ShapeDtypeStruct((len(group) * depth // INNER, width), jnp.bfloat16)
        for group in GROUPS
        for _ in range(2)
    ]
    outs += [jax.ShapeDtypeStruct((rows, width), jnp.float32)] * 2
    whole = pl.BlockSpec(memory_space=pltpu.VMEM)
    operands = [*own, *pieces, *others]
    return pl.pallas_call(
        functools.partial(solve_kernel, steps, block),
        out_shape=outs,
        in_specs=[whole] * len(operands),
        out_specs=[whole] * len(outs),
        scratch_shapes=[
            pltpu.VMEM((3, depth, depth), jnp.float32),
            pltpu.VMEM((depth, width), jnp.float32),
            pltpu.VMEM((depth, width), jnp.float32),
            pltpu.VMEM((2, depth, width), jnp.float32),
        ],
        compiler_params=pltpu.CompilerParams(vmem_limit_bytes=VMEM_BYTES),
        cost_estimate=COST,
    )(*operands)


def update_kernel(near_count, far_count, start, tile, *refs):
    near, refs = refs[:near_count], refs[near_count:]
    far, refs = refs[:far_count], refs[far_count:]
    near_factor, refs = (refs[:2], refs[2:]) if near else (None, refs)
    far_factor, refs = (refs[:2], refs[2:]) if far else (None, refs)
    before, after, work, arrived, left = refs
    tiles = work.shape[0] // tile
    full = far[0].shape[1] // tile if far else 0

    def rows_of(t, first=0):
        return pl.ds(pl.multiple_of(first + t * tile, tile), tile)

    def bring(t):
        return pltpu.make_async_copy(before.at[rows_of(t, start)], work.at[rows_of(t)], arrived.at[t])

    def take(t):
        return pltpu.make_async_copy(work.at[rows_of(t)], after.at[rows_of(t, start)], left.at[t])

    def part(panels, factor, t):
        panel = jnp.concatenate([ref[:, rows_of(t)] for ref in panels], axis=0)
        return product(split(panel), (factor[0][...], factor[1][...]), contract=0)

    def step(t, with_far):
        total = part(near, near_factor, t) if near else 0.0
        if with_far:
            total = total + part(far, far_factor, t)
        bring(t).wait()
        work[rows_of(t), :] = work[rows_of(t), :] - total
        take(t).start()

    for t in range(tiles):
        bring(t).start()
    pl.loop(0, full)(lambda t: step(t, True))
    if full < tiles:
        pl.loop(full, tiles)(lambda t: step(t, False))
    for t in range(tiles):
        take(t).wait()


def update(near, near_factor, far, far_factor, before, start, tile, in_place):
    rows, width = (near or far)[0].shape[1], before.shape[1]
    tile = min(tile, rows)
    operands = [*near, *far, *(near_factor if near else ()), *(far_factor if far else ())]
    anywhere = pl.BlockSpec(memory_space=pl.ANY)
    return pl.pallas_call(
        functools.partial(update_kernel, len(near), len(far), start, tile),
        out_shape=jax.ShapeDtypeStruct(before.shape, jnp.float32),
        in_specs=[pl.BlockSpec(memory_space=pltpu.VMEM)] * len(operands) + [anywhere],
        out_specs=anywhere,
        input_output_aliases={len(operands): 0} if in_place else {},
        scratch_shapes=[
            pltpu.VMEM((rows, width), jnp.float32),
            pltpu.SemaphoreType.DMA((rows // tile,)),
            pltpu.SemaphoreType.DMA((rows // tile,)),
        ],
        compiler_params=pltpu.CompilerParams(vmem_limit_bytes=UPDATE_BYTES),
        cost_estimate=COST,
    )(*operands, before)


def solution(mesh):
    row_count, col_count = mesh.shape["row"], mesh.shape["col"]

    def swap(value, bit):
        return lax.ppermute(value, "col", [(i, i ^ bit) for i in range(col_count)])

    def shift(value, by):
        return lax.ppermute(value, "row", [(i, (i + by) % row_count) for i in range(row_count)])

    def per_device(
        inverse_first, inverse_second, coupling, panel_first, panel_second,
        rhs_first, rhs_second, rhs_rest,
    ):
        first, second = panel_first.T, panel_second.T
        block = first.shape[0]
        if col_count > INNER:
            groups = [list(range(i, col_count, INNER)) for i in range(INNER)]
            first, second = (
                lax.all_gather(p, "col", axis=0, tiled=True, axis_index_groups=groups)
                for p in (first, second)
            )
        rest = first.shape[1]

        own = (inverse_first, inverse_second, coupling, rhs_first, rhs_second)
        def cross(value, masks):
            return lax.ppermute(value, "col", [(i, i ^ masks[i % 2]) for i in range(col_count)])

        def beside(pair):
            return tuple(swap(x, CORE) for x in pair)

        def after(values, *tokens):
            return lax.optimization_barrier((values, tokens))[0]

        near_0 = tuple(cross(x, ONE) for x in (first, second))
        own_beside = beside((first, second))
        matrix_rows = 3 * rhs_first.shape[0]
        packs = [shift(pack_rows(own), 1)]
        near_1 = tuple(cross(x, OTHER) for x in after((first, second), own_beside, packs[0]))
        for _ in range(row_count - 2):
            packs.append(shift(packs[-1], 1))
        beside_0 = swap(near_0[0], CORE)
        beside_0 = beside_0, swap(after(near_0[1], beside_0), CORE)
        early = swap(after(packs[0][:matrix_rows], near_1, beside_0), CORE)
        late = swap(after(jnp.concatenate([p[:matrix_rows] for p in packs[1:]], axis=0), early), CORE)
        others = [early, late]
        cuts = [0, rest // 4, rest // 2, rest]
        far = [
            cross(jnp.concatenate([x[:, a:b] for x in after(near_0, near_1)], axis=0), OTHER)
            for a, b in zip(cuts[:-1], cuts[1:])
        ]
        beside_1 = beside(near_1)
        near = [
            panel
            for pair in ((first, second), own_beside, near_0, beside_0, near_1, beside_1)
            for panel in pair
        ]
        *factors, solved_first, solved_second = solve(row_count, block, own, packs, after(others, beside_1))
        near_factor, far_factor = factors[:2], factors[2:]
        lead = [jnp.concatenate(x, axis=1) for x in (far[:2], [swap(panel, CORE) for panel in far[:2]])]
        updated = update(near, near_factor, lead, far_factor, rhs_rest, 0, 1024, False)
        for start, panel in zip(cuts[2:], far[2:]):
            panel = after(panel, updated)
            updated = update([], None, [panel, swap(panel, CORE)], far_factor, updated, start, 512, True)
        return solved_first, solved_second, updated

    in_specs = (P("row", None),) * 3 + (P("row", "col"),) * 5
    return jax.shard_map(
        per_device, mesh=mesh, in_specs=in_specs, out_specs=(P("row", "col"),) * 3, check_vma=False
    )
```

```python
import functools

import jax
import jax.numpy as jnp
from jax import lax
from jax.experimental import pallas as pl
from jax.experimental.pallas import tpu as pltpu
from jax.sharding import PartitionSpec as P

VMEM_BYTES = 24 * 2**20
UPDATE_BYTES = 32 * 2**20
COST = pl.CostEstimate(flops=1024, bytes_accessed=1024, transcendentals=0)
INNER = 8
CORE, ACROSS, UP = 1, 2, 4
FIRST, SECOND = 0, 1
ONE, OTHER = (ACROSS, UP), (UP, ACROSS)


def beyond(masks):
    return masks[1] | CORE, masks[0] | CORE


BOTH = (ACROSS | UP, ACROSS | UP)
GROUPS = tuple(
    tuple((panel, masks) for who in block for masks in (who, beyond(who)) for panel in (FIRST, SECOND))
    for block in (((0, 0), ONE, OTHER), (BOTH,))
)


def split(value):
    high = value.astype(jnp.bfloat16)
    return high, (value - high.astype(jnp.float32)).astype(jnp.bfloat16)


def product(left, right, contract=1):
    def one(a, b):
        return lax.dot_general(
            a, b, (((contract,), (0,)), ((), ())), preferred_element_type=jnp.float32
        )

    return one(left[0], right[0]) + one(left[0], right[1]) + one(left[1], right[0])


def pack_kernel(*refs):
    (*matrices, first, second), out = refs[:-1], refs[-1]
    rows, width = first.shape
    even = lax.rem(lax.axis_index("col"), 2) == 0
    for k, ref in enumerate(matrices):
        out[k * rows : (k + 1) * rows, :] = jnp.where(even, ref[:, :width], ref[:, width:])
    out[3 * rows : 4 * rows, :] = first[...]
    out[4 * rows :, :] = second[...]


def pack_rows(own):
    rows, width = own[3].shape
    whole = pl.BlockSpec(memory_space=pltpu.VMEM)
    return pl.pallas_call(
        pack_kernel,
        out_shape=jax.ShapeDtypeStruct((5 * rows, width), jnp.float32),
        in_specs=[whole] * 5,
        out_specs=whole,
        cost_estimate=COST,
    )(*own)


def solve_kernel(steps, block, *refs):
    own, refs = refs[:5], refs[5:]
    pieces, (early, late, *refs) = refs[: steps - 1], refs[steps - 1 :]
    outs, (first_out, second_out, *scratch) = refs[: 2 * len(GROUPS)], refs[2 * len(GROUPS) :]
    matrices, right_first, right_second, solved = scratch
    here = lax.axis_index("row")
    lane = lax.axis_index("col")
    even = lax.rem(lane, 2) == 0
    rows, width = own[3].shape[0], matrices.shape[2] // 2

    place = jnp.where(lax.rem(here, 2) == 0, here // 2, steps - (here + 1) // 2)

    def at(step):
        back = lax.rem(place + steps - step, steps)
        source = jnp.where(2 * back < steps, 2 * back, 2 * steps - 1 - 2 * back)
        return pl.ds(pl.multiple_of(source * rows, rows), rows)

    for k in range(3):
        matrices[k, at(0), :] = own[k][...]
    right_first[at(0), :] = own[3][...]
    right_second[at(0), :] = own[4][...]
    for j, piece in enumerate(pieces):
        right_first[at(j + 1), :] = piece[3 * rows : 4 * rows, :]
        right_second[at(j + 1), :] = piece[4 * rows :, :]
        for k in range(3):
            mine = piece[k * rows : (k + 1) * rows, :]
            others, at_row = (early, 3 * j + k) if j < steps - 2 else (late, k)
            other = others[at_row * rows : (at_row + 1) * rows, :]
            matrices[k, at(j + 1), :width] = jnp.where(even, mine, other)
            matrices[k, at(j + 1), width:] = jnp.where(even, other, mine)
    solved[0] = product(split(matrices[0]), split(right_first[...]))
    reduced = right_second[...] - product(split(matrices[2]), split(solved[0]))
    solved[1] = product(split(matrices[1]), split(reduced))
    first_out[...] = solved[0, at(0), :]
    second_out[...] = solved[1, at(0), :]

    inner = lax.rem(lane, INNER)
    outer = solved.shape[1] // (INNER * block)
    for group, (high_out, low_out) in zip(GROUPS, zip(outs[::2], outs[1::2])):
        to = 0
        for part, (mask, odd_mask) in group:
            which = lax.bitwise_xor(inner, jnp.where(even, mask, odd_mask))
            for o in range(outer):
                start = pl.multiple_of((o * INNER + which) * block, block)
                high, low = split(solved[part, pl.ds(start, block), :])
                high_out[to : to + block, :] = high
                low_out[to : to + block, :] = low
                to += block


def solve(steps, block, own, pieces, others):
    rows, width = own[3].shape
    depth = rows * steps
    outs = [
        jax.ShapeDtypeStruct((len(group) * depth // INNER, width), jnp.bfloat16)
        for group in GROUPS
        for _ in range(2)
    ]
    outs += [jax.ShapeDtypeStruct((rows, width), jnp.float32)] * 2
    whole = pl.BlockSpec(memory_space=pltpu.VMEM)
    operands = [*own, *pieces, *others]
    return pl.pallas_call(
        functools.partial(solve_kernel, steps, block),
        out_shape=outs,
        in_specs=[whole] * len(operands),
        out_specs=[whole] * len(outs),
        scratch_shapes=[
            pltpu.VMEM((3, depth, depth), jnp.float32),
            pltpu.VMEM((depth, width), jnp.float32),
            pltpu.VMEM((depth, width), jnp.float32),
            pltpu.VMEM((2, depth, width), jnp.float32),
        ],
        compiler_params=pltpu.CompilerParams(vmem_limit_bytes=VMEM_BYTES),
        cost_estimate=COST,
    )(*operands)


def update_kernel(near_count, far_count, start, tile, *refs):
    near, refs = refs[:near_count], refs[near_count:]
    far, refs = refs[:far_count], refs[far_count:]
    near_factor, refs = (refs[:2], refs[2:]) if near else (None, refs)
    far_factor, refs = (refs[:2], refs[2:]) if far else (None, refs)
    before, after, work, arrived, left = refs
    tiles = work.shape[0] // tile
    full = far[0].shape[1] // tile if far else 0

    def rows_of(t, first=0):
        return pl.ds(pl.multiple_of(first + t * tile, tile), tile)

    def bring(t):
        return pltpu.make_async_copy(before.at[rows_of(t, start)], work.at[rows_of(t)], arrived.at[t])

    def take(t):
        return pltpu.make_async_copy(work.at[rows_of(t)], after.at[rows_of(t, start)], left.at[t])

    def part(panels, factor, t):
        panel = jnp.concatenate([ref[:, rows_of(t)] for ref in panels], axis=0)
        return product(split(panel), (factor[0][...], factor[1][...]), contract=0)

    def step(t, with_far):
        total = part(near, near_factor, t) if near else 0.0
        if with_far:
            total = total + part(far, far_factor, t)
        bring(t).wait()
        work[rows_of(t), :] = work[rows_of(t), :] - total
        take(t).start()

    for t in range(tiles):
        bring(t).start()
    pl.loop(0, full)(lambda t: step(t, True))
    if full < tiles:
        pl.loop(full, tiles)(lambda t: step(t, False))
    for t in range(tiles):
        take(t).wait()


def update(near, near_factor, far, far_factor, before, start, tile, in_place):
    rows, width = (near or far)[0].shape[1], before.shape[1]
    tile = min(tile, rows)
    operands = [*near, *far, *(near_factor if near else ()), *(far_factor if far else ())]
    anywhere = pl.BlockSpec(memory_space=pl.ANY)
    return pl.pallas_call(
        functools.partial(update_kernel, len(near), len(far), start, tile),
        out_shape=jax.ShapeDtypeStruct(before.shape, jnp.float32),
        in_specs=[pl.BlockSpec(memory_space=pltpu.VMEM)] * len(operands) + [anywhere],
        out_specs=anywhere,
        input_output_aliases={len(operands): 0} if in_place else {},
        scratch_shapes=[
            pltpu.VMEM((rows, width), jnp.float32),
            pltpu.SemaphoreType.DMA((rows // tile,)),
            pltpu.SemaphoreType.DMA((rows // tile,)),
        ],
        compiler_params=pltpu.CompilerParams(vmem_limit_bytes=UPDATE_BYTES),
        cost_estimate=COST,
    )(*operands, before)


def solution(mesh):
    row_count, col_count = mesh.shape["row"], mesh.shape["col"]

    def swap(value, bit):
        return lax.ppermute(value, "col", [(i, i ^ bit) for i in range(col_count)])

    ring = [*range(0, row_count, 2), *reversed(range(1, row_count, 2))]

    def onward(value):
        return lax.ppermute(value, "row", list(zip(ring, ring[1:] + ring[:1])))

    def per_device(
        inverse_first, inverse_second, coupling, panel_first, panel_second,
        rhs_first, rhs_second, rhs_rest,
    ):
        first, second = panel_first.T, panel_second.T
        block = first.shape[0]
        if col_count > INNER:
            groups = [list(range(i, col_count, INNER)) for i in range(INNER)]
            first, second = (
                lax.all_gather(p, "col", axis=0, tiled=True, axis_index_groups=groups)
                for p in (first, second)
            )
        rest = first.shape[1]

        own = (inverse_first, inverse_second, coupling, rhs_first, rhs_second)
        def cross(value, masks):
            return lax.ppermute(value, "col", [(i, i ^ masks[i % 2]) for i in range(col_count)])

        def beside(pair):
            return tuple(swap(x, CORE) for x in pair)

        def after(values, *tokens):
            return lax.optimization_barrier((values, tokens))[0]

        near_0 = tuple(cross(x, ONE) for x in (first, second))
        own_beside = beside((first, second))
        matrix_rows = 3 * rhs_first.shape[0]
        packs = [onward(pack_rows(own))]
        near_1 = tuple(cross(x, OTHER) for x in after((first, second), own_beside, packs[0]))
        beside_0 = beside(near_0)
        for j in range(row_count - 2):
            packs.append(onward(after(packs[-1], beside_0[0]) if j == row_count - 3 else packs[-1]))
        cut = first.shape[0] // 2
        beside_1 = beside((near_1[0][:cut], near_1[0][cut:]))
        cuts = [0, rest // 2, rest]

        def far_part(pair, a, b):
            return cross(jnp.concatenate([x[:, a:b] for x in pair], axis=0), OTHER)

        far = [far_part(near_0, cuts[0], cuts[1])]
        early = swap(jnp.concatenate([p[:matrix_rows] for p in packs[:-1]], axis=0), CORE)
        near_0, near_1, beside_0, beside_1, packs, early = lax.optimization_barrier(
            (near_0, near_1, beside_0, beside_1, packs, early)
        )
        far += [far_part(near_0, a, b) for a, b in zip(cuts[1:-1], cuts[2:])]
        others = early, swap(packs[-1][:matrix_rows], CORE)
        beside_1 = *beside_1, swap(near_1[1], CORE)
        near = [
            panel
            for pair in ((first, second), own_beside, near_0, beside_0, near_1, beside_1)
            for panel in pair
        ]
        *factors, solved_first, solved_second = solve(row_count, block, own, packs, others)
        near_factor, far_factor = factors[:2], factors[2:]
        updated = update(near, near_factor, [far[0], swap(after(far[0], others), CORE)], far_factor, rhs_rest, 0, 1024, False)
        for start, panel in zip(cuts[1:], far[1:]):
            panel = after(panel, updated)
            updated = update([], None, [panel, swap(panel, CORE)], far_factor, updated, start, 512, True)
        return solved_first, solved_second, updated

    in_specs = (P("row", None),) * 3 + (P("row", "col"),) * 5
    return jax.shard_map(
        per_device, mesh=mesh, in_specs=in_specs, out_specs=(P("row", "col"),) * 3, check_vma=False
    )
```

```python
import functools

import jax
import jax.numpy as jnp
from jax import lax
from jax.experimental import pallas as pl
from jax.experimental.pallas import tpu as pltpu
from jax.sharding import PartitionSpec as P

VMEM_BYTES = 24 * 2**20
UPDATE_BYTES = 32 * 2**20
UPDATE_TILE, LAST_TILE = 1024, 1024
COST = pl.CostEstimate(flops=1024, bytes_accessed=1024, transcendentals=0)
INNER = 8
CORE, ACROSS, UP = 1, 2, 4
FIRST, SECOND = 0, 1
ONE, OTHER = (ACROSS, UP), (UP, ACROSS)


def beyond(masks):
    return masks[1] | CORE, masks[0] | CORE


BOTH = (ACROSS | UP, ACROSS | UP)
GROUPS = tuple(
    tuple((panel, masks) for who in block for masks in (who, beyond(who)) for panel in (FIRST, SECOND))
    for block in (((0, 0), ONE, OTHER), (BOTH,))
)


def split(value):
    high = value.astype(jnp.bfloat16)
    return high, (value - high.astype(jnp.float32)).astype(jnp.bfloat16)


def product(left, right, contract=1):
    def one(a, b):
        return lax.dot_general(
            a, b, (((contract,), (0,)), ((), ())), preferred_element_type=jnp.float32
        )

    return one(left[0], right[0]) + one(left[0], right[1]) + one(left[1], right[0])


def pack_kernel(*refs):
    (*matrices, first, second), out = refs[:-1], refs[-1]
    rows, width = first.shape
    even = lax.rem(lax.axis_index("col"), 2) == 0
    for k, ref in enumerate(matrices):
        out[k * rows : (k + 1) * rows, :] = jnp.where(even, ref[:, :width], ref[:, width:])
    out[3 * rows : 4 * rows, :] = first[...]
    out[4 * rows :, :] = second[...]


def pack_rows(own):
    rows, width = own[3].shape
    whole = pl.BlockSpec(memory_space=pltpu.VMEM)
    return pl.pallas_call(
        pack_kernel,
        out_shape=jax.ShapeDtypeStruct((5 * rows, width), jnp.float32),
        in_specs=[whole] * 5,
        out_specs=whole,
        cost_estimate=COST,
    )(*own)


def solve_kernel(steps, block, *refs):
    own, refs = refs[:5], refs[5:]
    pieces, (early, late, *refs) = refs[: steps - 1], refs[steps - 1 :]
    outs, (first_out, second_out, *scratch) = refs[: 2 * len(GROUPS)], refs[2 * len(GROUPS) :]
    matrices, right_first, right_second, solved = scratch
    here = lax.axis_index("row")
    lane = lax.axis_index("col")
    even = lax.rem(lane, 2) == 0
    rows, width = own[3].shape[0], matrices.shape[2] // 2

    place = jnp.where(lax.rem(here, 2) == 0, here // 2, steps - (here + 1) // 2)

    def at(step):
        back = lax.rem(place + steps - step, steps)
        source = jnp.where(2 * back < steps, 2 * back, 2 * steps - 1 - 2 * back)
        return pl.ds(pl.multiple_of(source * rows, rows), rows)

    for k in range(3):
        matrices[k, at(0), :] = own[k][...]
    right_first[at(0), :] = own[3][...]
    right_second[at(0), :] = own[4][...]
    for j, piece in enumerate(pieces):
        right_first[at(j + 1), :] = piece[3 * rows : 4 * rows, :]
        right_second[at(j + 1), :] = piece[4 * rows :, :]
        for k in range(3):
            mine = piece[k * rows : (k + 1) * rows, :]
            others, at_row = (early, 3 * j + k) if j < steps - 2 else (late, k)
            other = others[at_row * rows : (at_row + 1) * rows, :]
            matrices[k, at(j + 1), :width] = jnp.where(even, mine, other)
            matrices[k, at(j + 1), width:] = jnp.where(even, other, mine)
    solved[0] = product(split(matrices[0]), split(right_first[...]))
    reduced = right_second[...] - product(split(matrices[2]), split(solved[0]))
    solved[1] = product(split(matrices[1]), split(reduced))
    first_out[...] = solved[0, at(0), :]
    second_out[...] = solved[1, at(0), :]

    inner = lax.rem(lane, INNER)
    outer = solved.shape[1] // (INNER * block)
    for group, (high_out, low_out) in zip(GROUPS, zip(outs[::2], outs[1::2])):
        to = 0
        for part, (mask, odd_mask) in group:
            which = lax.bitwise_xor(inner, jnp.where(even, mask, odd_mask))
            for o in range(outer):
                start = pl.multiple_of((o * INNER + which) * block, block)
                high, low = split(solved[part, pl.ds(start, block), :])
                high_out[to : to + block, :] = high
                low_out[to : to + block, :] = low
                to += block


def solve(steps, block, own, pieces, others):
    rows, width = own[3].shape
    depth = rows * steps
    outs = [
        jax.ShapeDtypeStruct((len(group) * depth // INNER, width), jnp.bfloat16)
        for group in GROUPS
        for _ in range(2)
    ]
    outs += [jax.ShapeDtypeStruct((rows, width), jnp.float32)] * 2
    whole = pl.BlockSpec(memory_space=pltpu.VMEM)
    operands = [*own, *pieces, *others]
    return pl.pallas_call(
        functools.partial(solve_kernel, steps, block),
        out_shape=outs,
        in_specs=[whole] * len(operands),
        out_specs=[whole] * len(outs),
        scratch_shapes=[
            pltpu.VMEM((3, depth, depth), jnp.float32),
            pltpu.VMEM((depth, width), jnp.float32),
            pltpu.VMEM((depth, width), jnp.float32),
            pltpu.VMEM((2, depth, width), jnp.float32),
        ],
        compiler_params=pltpu.CompilerParams(vmem_limit_bytes=VMEM_BYTES),
        cost_estimate=COST,
    )(*operands)


def rows_of(t, tile, first=0):
    return pl.ds(pl.multiple_of(first + t * tile, tile), tile)


def turned_product(panels, factor, rows):
    panel = jnp.concatenate([ref[:, rows] for ref in panels], axis=0)
    return product(split(panel), factor, contract=0)


def update_kernel(near_count, far_count, tile, *refs):
    near, refs = refs[:near_count], refs[near_count:]
    far, refs = refs[:far_count], refs[far_count:]
    near_high, near_low, far_high, far_low, before, after, rest, work, arrived, left = refs
    full, tiles = work.shape[0] // tile, before.shape[0] // tile

    def bring(t, to, first):
        here = before.at[rows_of(t, tile), :]
        return pltpu.make_async_copy(here, to.at[rows_of(t - first, tile), :], arrived.at[t])

    def take(t):
        return pltpu.make_async_copy(work.at[rows_of(t, tile), :], after.at[rows_of(t, tile), :], left.at[t])

    for t in range(tiles):
        bring(t, work if t < full else rest, 0 if t < full else full).start()

    @pl.loop(0, full)
    def _(t):
        rows = rows_of(t, tile)
        total = turned_product(near, (near_high[...], near_low[...]), rows)
        total = total + turned_product(far, (far_high[...], far_low[...]), rows)
        bring(t, work, 0).wait()
        work[rows, :] = work[rows, :] - total
        take(t).start()

    @pl.loop(full, tiles)
    def _(t):
        total = turned_product(near, (near_high[...], near_low[...]), rows_of(t, tile))
        bring(t, rest, full).wait()
        rows = rows_of(t - full, tile)
        rest[rows, :] = rest[rows, :] - total

    for t in range(full):
        take(t).wait()


def update(near, near_factor, far, far_factor, before):
    rows, width, full = before.shape[0], before.shape[1], far[0].shape[1]
    tile = min(UPDATE_TILE, full)
    operands = [*near, *far, *near_factor, *far_factor]
    anywhere, inside = pl.BlockSpec(memory_space=pl.ANY), pl.BlockSpec(memory_space=pltpu.VMEM)
    return pl.pallas_call(
        functools.partial(update_kernel, len(near), len(far), tile),
        out_shape=[
            jax.ShapeDtypeStruct(before.shape, jnp.float32),
            jax.ShapeDtypeStruct((rows - full, width), jnp.float32),
        ],
        in_specs=[inside] * len(operands) + [anywhere],
        out_specs=[anywhere, inside],
        scratch_shapes=[
            pltpu.VMEM((full, width), jnp.float32),
            pltpu.SemaphoreType.DMA((rows // tile,)),
            pltpu.SemaphoreType.DMA((full // tile,)),
        ],
        compiler_params=pltpu.CompilerParams(vmem_limit_bytes=UPDATE_BYTES),
        cost_estimate=COST,
    )(*operands, before)


def subtract_kernel(tile, panel, high, low, before, after):
    @pl.loop(0, before.shape[0] // tile)
    def _(t):
        rows = rows_of(t, tile)
        half = pl.ds(0, panel.shape[0])
        after[rows, :] = before[rows, :] - turned_product([panel], (high[half, :], low[half, :]), rows)


def subtract(panel, factor, before):
    inside = pl.BlockSpec(memory_space=pltpu.VMEM)
    return pl.pallas_call(
        functools.partial(subtract_kernel, min(LAST_TILE, before.shape[0])),
        out_shape=jax.ShapeDtypeStruct(before.shape, jnp.float32),
        in_specs=[inside] * 4,
        out_specs=inside,
        input_output_aliases={3: 0},
        compiler_params=pltpu.CompilerParams(vmem_limit_bytes=VMEM_BYTES),
        cost_estimate=COST,
    )(panel, *factor, before)


def finish_kernel(tile, panel, high, low, rest, before, after, work, left):
    rows, start = rest.shape[0], after.shape[0] - rest.shape[0]

    def take(t):
        to = after.at[rows_of(t, tile, start), :]
        return pltpu.make_async_copy(work.at[rows_of(t, tile), :], to, left.at[t])

    @pl.loop(0, rows // tile)
    def _(t):
        here = rows_of(t, tile)
        half = pl.ds(panel.shape[0], panel.shape[0])
        work[here, :] = rest[here, :] - turned_product([panel], (high[half, :], low[half, :]), here)
        take(t).start()

    for t in range(rows // tile):
        take(t).wait()


def finish(panel, factor, rest, before):
    rows = rest.shape[0]
    tile = min(LAST_TILE, rows)
    anywhere, inside = pl.BlockSpec(memory_space=pl.ANY), pl.BlockSpec(memory_space=pltpu.VMEM)
    return pl.pallas_call(
        functools.partial(finish_kernel, tile),
        out_shape=jax.ShapeDtypeStruct(before.shape, jnp.float32),
        in_specs=[inside] * 4 + [anywhere],
        out_specs=anywhere,
        input_output_aliases={4: 0},
        scratch_shapes=[pltpu.VMEM(rest.shape, jnp.float32), pltpu.SemaphoreType.DMA((rows // tile,))],
        compiler_params=pltpu.CompilerParams(vmem_limit_bytes=VMEM_BYTES),
        cost_estimate=COST,
    )(panel, *factor, rest, before)


def solution(mesh):
    row_count, col_count = mesh.shape["row"], mesh.shape["col"]

    def swap(value, bit):
        return lax.ppermute(value, "col", [(i, i ^ bit) for i in range(col_count)])

    ring = [*range(0, row_count, 2), *reversed(range(1, row_count, 2))]

    def onward(value):
        return lax.ppermute(value, "row", list(zip(ring, ring[1:] + ring[:1])))

    def per_device(
        inverse_first, inverse_second, coupling, panel_first, panel_second,
        rhs_first, rhs_second, rhs_rest,
    ):
        first, second = panel_first.T, panel_second.T
        block = first.shape[0]
        if col_count > INNER:
            groups = [list(range(i, col_count, INNER)) for i in range(INNER)]
            first, second = (
                lax.all_gather(p, "col", axis=0, tiled=True, axis_index_groups=groups)
                for p in (first, second)
            )
        rest = first.shape[1]

        own = (inverse_first, inverse_second, coupling, rhs_first, rhs_second)
        def cross(value, masks):
            return lax.ppermute(value, "col", [(i, i ^ masks[i % 2]) for i in range(col_count)])

        def beside(pair):
            return tuple(swap(x, CORE) for x in pair)

        def halves(value):
            return jnp.split(value, 2, axis=0)

        def after(values, *tokens):
            return lax.optimization_barrier((values, tokens))[0]

        near_0 = tuple(cross(x, ONE) for x in (first, second))
        own_beside = beside((first, second))
        matrix_rows = 3 * rhs_first.shape[0]
        packs = [onward(pack_rows(own))]
        near_1 = tuple(cross(x, OTHER) for x in after((first, second), own_beside, packs[0]))
        beside_0 = beside(near_0)
        for j in range(row_count - 2):
            packs.append(onward(after(packs[-1], beside_0[0]) if j == row_count - 3 else packs[-1]))
        beside_1 = beside(halves(near_1[0]))
        cuts = [0, rest // 2, rest]

        def far_part(pair, a, b):
            return cross(jnp.concatenate([x[:, a:b] for x in pair], axis=0), OTHER)

        far = [far_part(near_0, cuts[0], cuts[1])]
        early = swap(jnp.concatenate([p[:matrix_rows] for p in packs[:-1]], axis=0), CORE)
        near_0, near_1, beside_0, beside_1, packs, early = lax.optimization_barrier(
            (near_0, near_1, beside_0, beside_1, packs, early)
        )
        far += [far_part(near_0, a, b) for a, b in zip(cuts[1:-1], cuts[2:])]
        others = early, swap(packs[-1][:matrix_rows], CORE)
        beside_1 += beside(halves(after(near_1[1], others)))
        near = [
            panel
            for pair in ((first, second), own_beside, near_0, beside_0, near_1, beside_1)
            for panel in pair
        ]
        *factors, solved_first, solved_second = solve(row_count, block, own, packs, others)
        near_factor, far_factor = factors[:2], factors[2:]
        near_far = [far[0], *beside(halves(after(far[0], others)))]
        updated, last = update(near, near_factor, near_far, far_factor, rhs_rest)
        panel = after(far[1], updated)
        other = swap(panel, CORE)
        updated = finish(other, far_factor, subtract(panel, far_factor, last), updated)
        return solved_first, solved_second, updated

    in_specs = (P("row", None),) * 3 + (P("row", "col"),) * 5
    return jax.shard_map(
        per_device, mesh=mesh, in_specs=in_specs, out_specs=(P("row", "col"),) * 3, check_vma=False
    )
```

```python
import functools

import jax
import jax.numpy as jnp
from jax import lax
from jax.experimental import pallas as pl
from jax.experimental.pallas import tpu as pltpu
from jax.sharding import PartitionSpec as P

VMEM_BYTES = 24 * 2**20
UPDATE_BYTES = 32 * 2**20
UPDATE_TILE, LAST_TILE = 1024, 512
COST = pl.CostEstimate(flops=1024, bytes_accessed=1024, transcendentals=0)
INNER = 8
CORE, ACROSS, UP = 1, 2, 4
FIRST, SECOND = 0, 1
ONE, OTHER = (ACROSS, UP), (UP, ACROSS)


def beyond(masks):
    return masks[1] | CORE, masks[0] | CORE


BOTH = (ACROSS | UP, ACROSS | UP)
GROUPS = tuple(
    tuple((panel, masks) for who in block for masks in (who, beyond(who)) for panel in (FIRST, SECOND))
    for block in (((0, 0), ONE, OTHER), (BOTH,))
)


def split(value):
    high = value.astype(jnp.bfloat16)
    return high, (value - high.astype(jnp.float32)).astype(jnp.bfloat16)


def product(left, right, contract=1):
    def one(a, b):
        return lax.dot_general(
            a, b, (((contract,), (0,)), ((), ())), preferred_element_type=jnp.float32
        )

    return one(left[0], right[0]) + one(left[0], right[1]) + one(left[1], right[0])


def pack_kernel(*refs):
    (*matrices, first, second), out = refs[:-1], refs[-1]
    rows, width = first.shape
    even = lax.rem(lax.axis_index("col"), 2) == 0
    for k, ref in enumerate(matrices):
        out[k * rows : (k + 1) * rows, :] = jnp.where(even, ref[:, :width], ref[:, width:])
    out[3 * rows : 4 * rows, :] = first[...]
    out[4 * rows :, :] = second[...]


def pack_rows(own):
    rows, width = own[3].shape
    whole = pl.BlockSpec(memory_space=pltpu.VMEM)
    return pl.pallas_call(
        pack_kernel,
        out_shape=jax.ShapeDtypeStruct((5 * rows, width), jnp.float32),
        in_specs=[whole] * 5,
        out_specs=whole,
        cost_estimate=COST,
    )(*own)


def solve_kernel(steps, block, *refs):
    own, refs = refs[:5], refs[5:]
    pieces, (early, late, *refs) = refs[: steps - 1], refs[steps - 1 :]
    outs, (first_out, second_out, *scratch) = refs[: 2 * len(GROUPS)], refs[2 * len(GROUPS) :]
    matrices, right_first, right_second, solved, current = scratch
    here = lax.axis_index("row")
    lane = lax.axis_index("col")
    even = lax.rem(lane, 2) == 0
    rows, width = own[3].shape[0], matrices.shape[2] // 2

    place = jnp.where(lax.rem(here, 2) == 0, here // 2, steps - (here + 1) // 2)

    def at(step):
        back = lax.rem(place + steps - step, steps)
        source = jnp.where(2 * back < steps, 2 * back, 2 * steps - 1 - 2 * back)
        return pl.ds(pl.multiple_of(source * rows, rows), rows)

    for k in range(3):
        matrices[k, at(0), :] = own[k][...]
    right_first[at(0), :] = own[3][...]
    right_second[at(0), :] = own[4][...]
    for j, piece in enumerate(pieces):
        right_first[at(j + 1), :] = piece[3 * rows : 4 * rows, :]
        right_second[at(j + 1), :] = piece[4 * rows :, :]
        for k in range(3):
            mine = piece[k * rows : (k + 1) * rows, :]
            others, at_row = (early, 3 * j + k) if j < steps - 2 else (late, k)
            other = others[at_row * rows : (at_row + 1) * rows, :]
            matrices[k, at(j + 1), :width] = jnp.where(even, mine, other)
            matrices[k, at(j + 1), width:] = jnp.where(even, other, mine)
    current[...] = right_first[...]

    @pl.loop(0, 3)
    def _(k):
        result = product(split(matrices[k]), split(current[...]))
        solved[k] = result
        current[...] = jnp.where(k == 1, right_second[...] - result, result)

    first_out[...] = solved[0, at(0), :]
    second_out[...] = solved[2, at(0), :]

    inner = lax.rem(lane, INNER)
    outer = solved.shape[1] // (INNER * block)
    for group, (high_out, low_out) in zip(GROUPS, zip(outs[::2], outs[1::2])):
        to = 0
        for part, (mask, odd_mask) in group:
            which = lax.bitwise_xor(inner, jnp.where(even, mask, odd_mask))
            for o in range(outer):
                start = pl.multiple_of((o * INNER + which) * block, block)
                high, low = split(solved[2 * part, pl.ds(start, block), :])
                high_out[to : to + block, :] = high
                low_out[to : to + block, :] = low
                to += block


def solve(steps, block, own, pieces, others):
    rows, width = own[3].shape
    depth = rows * steps
    outs = [
        jax.ShapeDtypeStruct((len(group) * depth // INNER, width), jnp.bfloat16)
        for group in GROUPS
        for _ in range(2)
    ]
    outs += [jax.ShapeDtypeStruct((rows, width), jnp.float32)] * 2
    whole = pl.BlockSpec(memory_space=pltpu.VMEM)
    operands = [*own, *pieces, *others]
    return pl.pallas_call(
        functools.partial(solve_kernel, steps, block),
        out_shape=outs,
        in_specs=[whole] * len(operands),
        out_specs=[whole] * len(outs),
        scratch_shapes=[
            pltpu.VMEM((3, depth, depth), jnp.float32),
            pltpu.VMEM((depth, width), jnp.float32),
            pltpu.VMEM((depth, width), jnp.float32),
            pltpu.VMEM((3, depth, width), jnp.float32),
            pltpu.VMEM((depth, width), jnp.float32),
        ],
        compiler_params=pltpu.CompilerParams(vmem_limit_bytes=VMEM_BYTES),
        cost_estimate=COST,
    )(*operands)


def rows_of(t, tile, first=0):
    if isinstance(t, int):
        return pl.ds(first + t * tile, tile)
    return pl.ds(pl.multiple_of(first + t * tile, tile), tile)


def turned_product(panels, factor, rows):
    panel = jnp.concatenate([ref[:, rows] for ref in panels], axis=0)
    return product(split(panel), factor, contract=0)


def update_kernel(near_count, far_count, tile, *refs):
    near, refs = refs[:near_count], refs[near_count:]
    far, refs = refs[:far_count], refs[far_count:]
    near_high, near_low, far_high, far_low, before, after, rest, work, arrived, left = refs
    full, tiles = work.shape[0] // tile, before.shape[0] // tile

    def bring(t, to, first):
        here = before.at[rows_of(t, tile), :]
        return pltpu.make_async_copy(here, to.at[rows_of(t - first, tile), :], arrived.at[t])

    def take(t):
        return pltpu.make_async_copy(work.at[rows_of(t, tile), :], after.at[rows_of(t, tile), :], left.at[t])

    for t in range(tiles):
        bring(t, work if t < full else rest, 0 if t < full else full).start()

    @pl.loop(0, full)
    def _(t):
        rows = rows_of(t, tile)
        total = turned_product(near, (near_high[...], near_low[...]), rows)
        total = total + turned_product(far, (far_high[...], far_low[...]), rows)
        bring(t, work, 0).wait()
        work[rows, :] = work[rows, :] - total
        take(t).start()

    @pl.loop(full, tiles)
    def _(t):
        total = turned_product(near, (near_high[...], near_low[...]), rows_of(t, tile))
        bring(t, rest, full).wait()
        rows = rows_of(t - full, tile)
        rest[rows, :] = rest[rows, :] - total

    for t in range(full):
        take(t).wait()


def update(near, near_factor, far, far_factor, before):
    rows, width, full = before.shape[0], before.shape[1], far[0].shape[1]
    tile = min(UPDATE_TILE, full)
    operands = [*near, *far, *near_factor, *far_factor]
    anywhere, inside = pl.BlockSpec(memory_space=pl.ANY), pl.BlockSpec(memory_space=pltpu.VMEM)
    return pl.pallas_call(
        functools.partial(update_kernel, len(near), len(far), tile),
        out_shape=[
            jax.ShapeDtypeStruct(before.shape, jnp.float32),
            jax.ShapeDtypeStruct((rows - full, width), jnp.float32),
        ],
        in_specs=[inside] * len(operands) + [anywhere],
        out_specs=[anywhere, inside],
        scratch_shapes=[
            pltpu.VMEM((full, width), jnp.float32),
            pltpu.SemaphoreType.DMA((rows // tile,)),
            pltpu.SemaphoreType.DMA((full // tile,)),
        ],
        compiler_params=pltpu.CompilerParams(vmem_limit_bytes=UPDATE_BYTES),
        cost_estimate=COST,
    )(*operands, before)


def subtract_kernel(tile, panel, high, low, before, after):
    @pl.loop(0, before.shape[0] // tile)
    def _(t):
        rows = rows_of(t, tile)
        half = pl.ds(0, panel.shape[0])
        after[rows, :] = before[rows, :] - turned_product([panel], (high[half, :], low[half, :]), rows)


def subtract(panel, factor, before):
    inside = pl.BlockSpec(memory_space=pltpu.VMEM)
    return pl.pallas_call(
        functools.partial(subtract_kernel, min(LAST_TILE, before.shape[0])),
        out_shape=jax.ShapeDtypeStruct(before.shape, jnp.float32),
        in_specs=[inside] * 4,
        out_specs=inside,
        input_output_aliases={3: 0},
        compiler_params=pltpu.CompilerParams(vmem_limit_bytes=VMEM_BYTES),
        cost_estimate=COST,
    )(panel, *factor, before)


def finish_kernel(tile, panel, high, low, rest, before, after, work, left):
    rows, start = rest.shape[0], after.shape[0] - rest.shape[0]

    def take(t):
        to = after.at[rows_of(t, tile, start), :]
        return pltpu.make_async_copy(work.at[rows_of(t, tile), :], to, left.at[t])

    for t in range(rows // tile):
        here = rows_of(t, tile)
        half = pl.ds(panel.shape[0], panel.shape[0])
        work[here, :] = rest[here, :] - turned_product([panel], (high[half, :], low[half, :]), here)
        take(t).start()
    for t in range(rows // tile):
        take(t).wait()


def finish(panel, factor, rest, before):
    rows = rest.shape[0]
    tile = min(LAST_TILE, rows)
    anywhere, inside = pl.BlockSpec(memory_space=pl.ANY), pl.BlockSpec(memory_space=pltpu.VMEM)
    return pl.pallas_call(
        functools.partial(finish_kernel, tile),
        out_shape=jax.ShapeDtypeStruct(before.shape, jnp.float32),
        in_specs=[inside] * 4 + [anywhere],
        out_specs=anywhere,
        input_output_aliases={4: 0},
        scratch_shapes=[pltpu.VMEM(rest.shape, jnp.float32), pltpu.SemaphoreType.DMA((rows // tile,))],
        compiler_params=pltpu.CompilerParams(vmem_limit_bytes=VMEM_BYTES),
        cost_estimate=COST,
    )(panel, *factor, rest, before)


def solution(mesh):
    row_count, col_count = mesh.shape["row"], mesh.shape["col"]

    def swap(value, bit):
        return lax.ppermute(value, "col", [(i, i ^ bit) for i in range(col_count)])

    ring = [*range(0, row_count, 2), *reversed(range(1, row_count, 2))]

    def onward(value):
        return lax.ppermute(value, "row", list(zip(ring, ring[1:] + ring[:1])))

    def per_device(
        inverse_first, inverse_second, coupling, panel_first, panel_second,
        rhs_first, rhs_second, rhs_rest,
    ):
        first, second = panel_first.T, panel_second.T
        block = first.shape[0]
        if col_count > INNER:
            groups = [list(range(i, col_count, INNER)) for i in range(INNER)]
            first, second = (
                lax.all_gather(p, "col", axis=0, tiled=True, axis_index_groups=groups)
                for p in (first, second)
            )
        rest = first.shape[1]

        own = (inverse_first, coupling, inverse_second, rhs_first, rhs_second)
        def cross(value, masks):
            return lax.ppermute(value, "col", [(i, i ^ masks[i % 2]) for i in range(col_count)])

        def beside(pair):
            return tuple(swap(x, CORE) for x in pair)

        def halves(value):
            return jnp.split(value, 2, axis=0)

        def after(values, *tokens):
            return lax.optimization_barrier((values, tokens))[0]

        near_0 = tuple(cross(x, ONE) for x in (first, second))
        own_beside = beside((first, second))
        matrix_rows = 3 * rhs_first.shape[0]
        packs = [onward(pack_rows(own))]
        near_1 = tuple(cross(x, OTHER) for x in after((first, second), own_beside, packs[0]))
        beside_0 = beside(near_0)
        for j in range(row_count - 2):
            packs.append(onward(after(packs[-1], beside_0[0]) if j == row_count - 3 else packs[-1]))
        beside_1 = beside(halves(near_1[0]))
        cuts = [0, rest // 2, rest]

        def far_part(pair, a, b):
            return cross(jnp.concatenate([x[:, a:b] for x in pair], axis=0), OTHER)

        far = [far_part(near_0, cuts[0], cuts[1])]
        early = swap(jnp.concatenate([p[:matrix_rows] for p in packs[:-1]], axis=0), CORE)
        near_0, near_1, beside_0, beside_1, packs, early = lax.optimization_barrier(
            (near_0, near_1, beside_0, beside_1, packs, early)
        )
        far += [far_part(near_0, a, b) for a, b in zip(cuts[1:-1], cuts[2:])]
        others = early, swap(packs[-1][:matrix_rows], CORE)
        beside_1 += beside(halves(after(near_1[1], others)))
        near = [
            panel
            for pair in ((first, second), own_beside, near_0, beside_0, near_1, beside_1)
            for panel in pair
        ]
        *factors, solved_first, solved_second = solve(row_count, block, own, packs, others)
        near_factor, far_factor = factors[:2], factors[2:]
        near_far = [far[0], *beside(halves(after(far[0], others)))]
        updated, last = update(near, near_factor, near_far, far_factor, rhs_rest)
        panel = after(far[1], updated)
        other = swap(panel, CORE)
        updated = finish(other, far_factor, subtract(panel, far_factor, last), updated)
        return solved_first, solved_second, updated

    in_specs = (P("row", None),) * 3 + (P("row", "col"),) * 5
    return jax.shard_map(
        per_device, mesh=mesh, in_specs=in_specs, out_specs=(P("row", "col"),) * 3, check_vma=False
    )
```

```python
import functools

import jax
import jax.numpy as jnp
from jax import lax
from jax.experimental import pallas as pl
from jax.experimental.pallas import tpu as pltpu
from jax.sharding import PartitionSpec as P

VMEM_BYTES = 24 * 2**20
UPDATE_BYTES = 32 * 2**20
UPDATE_TILE, LAST_TILE = 1024, 512
COST = pl.CostEstimate(flops=1024, bytes_accessed=1024, transcendentals=0)
INNER = 8
CORE, ACROSS, UP = 1, 2, 4
FIRST, SECOND = 0, 1
ONE, OTHER = (ACROSS, UP), (UP, ACROSS)


def beyond(masks):
    return masks[1] | CORE, masks[0] | CORE


BOTH = (ACROSS | UP, ACROSS | UP)
GROUPS = tuple(
    tuple((panel, masks) for who in block for masks in (who, beyond(who)) for panel in (FIRST, SECOND))
    for block in (((0, 0), ONE, OTHER), (BOTH,))
)


def split(value):
    high = value.astype(jnp.bfloat16)
    return high, (value - high.astype(jnp.float32)).astype(jnp.bfloat16)


def product(left, right, contract=1):
    def one(a, b):
        return lax.dot_general(
            a, b, (((contract,), (0,)), ((), ())), preferred_element_type=jnp.float32
        )

    return one(left[0], right[0]) + one(left[0], right[1]) + one(left[1], right[0])


def pack_kernel(*refs):
    (*matrices, first, second), out = refs[:-1], refs[-1]
    rows, width = first.shape
    even = lax.rem(lax.axis_index("col"), 2) == 0
    for k, ref in enumerate(matrices):
        out[k * rows : (k + 1) * rows, :] = jnp.where(even, ref[:, :width], ref[:, width:])
    out[3 * rows : 4 * rows, :] = first[...]
    out[4 * rows :, :] = second[...]


def pack_rows(own):
    rows, width = own[3].shape
    whole = pl.BlockSpec(memory_space=pltpu.VMEM)
    return pl.pallas_call(
        pack_kernel,
        out_shape=jax.ShapeDtypeStruct((5 * rows, width), jnp.float32),
        in_specs=[whole] * 5,
        out_specs=whole,
        cost_estimate=COST,
    )(*own)


def solve_kernel(steps, block, *refs):
    own, refs = refs[:5], refs[5:]
    pieces, (early, late, *refs) = refs[: steps - 1], refs[steps - 1 :]
    outs, (first_out, second_out, *scratch) = refs[: 2 * len(GROUPS)], refs[2 * len(GROUPS) :]
    matrices, right_first, right_second, solved, current = scratch
    here = lax.axis_index("row")
    lane = lax.axis_index("col")
    even = lax.rem(lane, 2) == 0
    rows, width = own[3].shape[0], matrices.shape[2] // 2

    place = jnp.where(lax.rem(here, 2) == 0, here // 2, steps - (here + 1) // 2)

    def at(step):
        back = lax.rem(place + steps - step, steps)
        source = jnp.where(2 * back < steps, 2 * back, 2 * steps - 1 - 2 * back)
        return pl.ds(pl.multiple_of(source * rows, rows), rows)

    for k in range(3):
        matrices[k, at(0), :] = own[k][...]
    right_first[at(0), :] = own[3][...]
    right_second[at(0), :] = own[4][...]
    for j, piece in enumerate(pieces):
        right_first[at(j + 1), :] = piece[3 * rows : 4 * rows, :]
        right_second[at(j + 1), :] = piece[4 * rows :, :]
        for k in range(3):
            mine = piece[k * rows : (k + 1) * rows, :]
            others, at_row = (early, 3 * j + k) if j < steps - 2 else (late, k)
            other = others[at_row * rows : (at_row + 1) * rows, :]
            matrices[k, at(j + 1), :width] = jnp.where(even, mine, other)
            matrices[k, at(j + 1), width:] = jnp.where(even, other, mine)
    current[...] = right_first[...]

    @pl.loop(0, 3)
    def _(k):
        result = product(split(matrices[k]), split(current[...]))
        solved[k] = result
        current[...] = jnp.where(k == 1, right_second[...] - result, result)

    first_out[...] = solved[0, at(0), :]
    second_out[...] = solved[2, at(0), :]

    inner = lax.rem(lane, INNER)
    outer = solved.shape[1] // (INNER * block)
    for group, (high_out, low_out) in zip(GROUPS, zip(outs[::2], outs[1::2])):
        to = 0
        for part, (mask, odd_mask) in group:
            which = lax.bitwise_xor(inner, jnp.where(even, mask, odd_mask))
            for o in range(outer):
                start = pl.multiple_of((o * INNER + which) * block, block)
                high, low = split(solved[2 * part, pl.ds(start, block), :])
                high_out[to : to + block, :] = high
                low_out[to : to + block, :] = low
                to += block


def solve(steps, block, own, pieces, others):
    rows, width = own[3].shape
    depth = rows * steps
    outs = [
        jax.ShapeDtypeStruct((len(group) * depth // INNER, width), jnp.bfloat16)
        for group in GROUPS
        for _ in range(2)
    ]
    outs += [jax.ShapeDtypeStruct((rows, width), jnp.float32)] * 2
    whole = pl.BlockSpec(memory_space=pltpu.VMEM)
    operands = [*own, *pieces, *others]
    return pl.pallas_call(
        functools.partial(solve_kernel, steps, block),
        out_shape=outs,
        in_specs=[whole] * len(operands),
        out_specs=[whole] * len(outs),
        scratch_shapes=[
            pltpu.VMEM((3, depth, depth), jnp.float32),
            pltpu.VMEM((depth, width), jnp.float32),
            pltpu.VMEM((depth, width), jnp.float32),
            pltpu.VMEM((3, depth, width), jnp.float32),
            pltpu.VMEM((depth, width), jnp.float32),
        ],
        compiler_params=pltpu.CompilerParams(vmem_limit_bytes=VMEM_BYTES),
        cost_estimate=COST,
    )(*operands)


def rows_of(t, tile, first=0):
    if isinstance(t, int):
        return pl.ds(first + t * tile, tile)
    return pl.ds(pl.multiple_of(first + t * tile, tile), tile)


def turned_product(panels, factor, rows):
    high, low = split(jnp.concatenate([ref[:, rows] for ref in panels], axis=0))
    left = jnp.concatenate([high, high, low], axis=0)
    right = jnp.concatenate([factor[0], factor[1], factor[0]], axis=0)
    return lax.dot_general(left, right, (((0,), (0,)), ((), ())), preferred_element_type=jnp.float32)


def update_kernel(near_count, far_count, tile, *refs):
    near, refs = refs[:near_count], refs[near_count:]
    far, refs = refs[:far_count], refs[far_count:]
    near_high, near_low, far_high, far_low, before, after, rest, work, arrived, left = refs
    full, tiles = work.shape[0] // tile, before.shape[0] // tile

    def bring(t, to, first):
        here = before.at[rows_of(t, tile), :]
        return pltpu.make_async_copy(here, to.at[rows_of(t - first, tile), :], arrived.at[t])

    def take(t):
        return pltpu.make_async_copy(work.at[rows_of(t, tile), :], after.at[rows_of(t, tile), :], left.at[t])

    for t in range(tiles):
        bring(t, work if t < full else rest, 0 if t < full else full).start()

    @pl.loop(0, full)
    def _(t):
        rows = rows_of(t, tile)
        total = turned_product(near, (near_high[...], near_low[...]), rows)
        total = total + turned_product(far, (far_high[...], far_low[...]), rows)
        bring(t, work, 0).wait()
        work[rows, :] = work[rows, :] - total
        take(t).start()

    @pl.loop(full, tiles)
    def _(t):
        total = turned_product(near, (near_high[...], near_low[...]), rows_of(t, tile))
        bring(t, rest, full).wait()
        rows = rows_of(t - full, tile)
        rest[rows, :] = rest[rows, :] - total

    for t in range(full):
        take(t).wait()


def update(near, near_factor, far, far_factor, before):
    rows, width, full = before.shape[0], before.shape[1], far[0].shape[1]
    tile = min(UPDATE_TILE, full)
    operands = [*near, *far, *near_factor, *far_factor]
    anywhere, inside = pl.BlockSpec(memory_space=pl.ANY), pl.BlockSpec(memory_space=pltpu.VMEM)
    return pl.pallas_call(
        functools.partial(update_kernel, len(near), len(far), tile),
        out_shape=[
            jax.ShapeDtypeStruct(before.shape, jnp.float32),
            jax.ShapeDtypeStruct((rows - full, width), jnp.float32),
        ],
        in_specs=[inside] * len(operands) + [anywhere],
        out_specs=[anywhere, inside],
        scratch_shapes=[
            pltpu.VMEM((full, width), jnp.float32),
            pltpu.SemaphoreType.DMA((rows // tile,)),
            pltpu.SemaphoreType.DMA((full // tile,)),
        ],
        compiler_params=pltpu.CompilerParams(vmem_limit_bytes=UPDATE_BYTES),
        cost_estimate=COST,
    )(*operands, before)


def subtract_kernel(tile, panel, high, low, before, after):
    @pl.loop(0, before.shape[0] // tile)
    def _(t):
        rows = rows_of(t, tile)
        half = pl.ds(0, panel.shape[0])
        after[rows, :] = before[rows, :] - turned_product([panel], (high[half, :], low[half, :]), rows)


def subtract(panel, factor, before):
    inside = pl.BlockSpec(memory_space=pltpu.VMEM)
    return pl.pallas_call(
        functools.partial(subtract_kernel, min(LAST_TILE, before.shape[0])),
        out_shape=jax.ShapeDtypeStruct(before.shape, jnp.float32),
        in_specs=[inside] * 4,
        out_specs=inside,
        input_output_aliases={3: 0},
        compiler_params=pltpu.CompilerParams(vmem_limit_bytes=VMEM_BYTES),
        cost_estimate=COST,
    )(panel, *factor, before)


def finish_kernel(tile, panel, high, low, rest, before, after, work, left):
    rows, start = rest.shape[0], after.shape[0] - rest.shape[0]

    def take(t):
        to = after.at[rows_of(t, tile, start), :]
        return pltpu.make_async_copy(work.at[rows_of(t, tile), :], to, left.at[t])

    for t in range(rows // tile):
        here = rows_of(t, tile)
        half = pl.ds(panel.shape[0], panel.shape[0])
        work[here, :] = rest[here, :] - turned_product([panel], (high[half, :], low[half, :]), here)
        take(t).start()
    for t in range(rows // tile):
        take(t).wait()


def finish(panel, factor, rest, before):
    rows = rest.shape[0]
    tile = min(LAST_TILE, rows)
    anywhere, inside = pl.BlockSpec(memory_space=pl.ANY), pl.BlockSpec(memory_space=pltpu.VMEM)
    return pl.pallas_call(
        functools.partial(finish_kernel, tile),
        out_shape=jax.ShapeDtypeStruct(before.shape, jnp.float32),
        in_specs=[inside] * 4 + [anywhere],
        out_specs=anywhere,
        input_output_aliases={4: 0},
        scratch_shapes=[pltpu.VMEM(rest.shape, jnp.float32), pltpu.SemaphoreType.DMA((rows // tile,))],
        compiler_params=pltpu.CompilerParams(vmem_limit_bytes=VMEM_BYTES),
        cost_estimate=COST,
    )(panel, *factor, rest, before)


def solution(mesh):
    row_count, col_count = mesh.shape["row"], mesh.shape["col"]

    def swap(value, bit):
        return lax.ppermute(value, "col", [(i, i ^ bit) for i in range(col_count)])

    ring = [*range(0, row_count, 2), *reversed(range(1, row_count, 2))]

    def onward(value):
        return lax.ppermute(value, "row", list(zip(ring, ring[1:] + ring[:1])))

    def per_device(
        inverse_first, inverse_second, coupling, panel_first, panel_second,
        rhs_first, rhs_second, rhs_rest,
    ):
        first, second = panel_first.T, panel_second.T
        block = first.shape[0]
        if col_count > INNER:
            groups = [list(range(i, col_count, INNER)) for i in range(INNER)]
            first, second = (
                lax.all_gather(p, "col", axis=0, tiled=True, axis_index_groups=groups)
                for p in (first, second)
            )
        rest = first.shape[1]

        own = (inverse_first, coupling, inverse_second, rhs_first, rhs_second)
        def cross(value, masks):
            return lax.ppermute(value, "col", [(i, i ^ masks[i % 2]) for i in range(col_count)])

        def beside(pair):
            return tuple(swap(x, CORE) for x in pair)

        def halves(value):
            return jnp.split(value, 2, axis=0)

        def after(values, *tokens):
            return lax.optimization_barrier((values, tokens))[0]

        near_0 = tuple(cross(x, ONE) for x in (first, second))
        own_beside = beside((first, second))
        matrix_rows = 3 * rhs_first.shape[0]
        packs = [onward(pack_rows(own))]
        near_1 = tuple(cross(x, OTHER) for x in after((first, second), own_beside, packs[0]))
        beside_0 = beside(near_0)
        for j in range(row_count - 2):
            packs.append(onward(after(packs[-1], beside_0[0]) if j == row_count - 3 else packs[-1]))
        beside_1 = beside(halves(near_1[0]))
        cuts = [0, rest // 2, rest]

        def far_part(pair, a, b):
            return cross(jnp.concatenate([x[:, a:b] for x in pair], axis=0), OTHER)

        far = [far_part(near_0, cuts[0], cuts[1])]
        early = swap(jnp.concatenate([p[:matrix_rows] for p in packs[:-1]], axis=0), CORE)
        near_0, near_1, beside_0, beside_1, packs, early = lax.optimization_barrier(
            (near_0, near_1, beside_0, beside_1, packs, early)
        )
        far += [far_part(near_0, a, b) for a, b in zip(cuts[1:-1], cuts[2:])]
        others = early, swap(packs[-1][:matrix_rows], CORE)
        beside_1 += beside(halves(after(near_1[1], others)))
        near = [
            panel
            for pair in ((first, second), own_beside, near_0, beside_0, near_1, beside_1)
            for panel in pair
        ]
        *factors, solved_first, solved_second = solve(row_count, block, own, packs, others)
        near_factor, far_factor = factors[:2], factors[2:]
        near_far = [far[0], *beside(halves(after(far[0], others)))]
        updated, last = update(near, near_factor, near_far, far_factor, rhs_rest)
        panel = after(far[1], updated)
        other = swap(panel, CORE)
        updated = finish(other, far_factor, subtract(panel, far_factor, last), updated)
        return solved_first, solved_second, updated

    in_specs = (P("row", None),) * 3 + (P("row", "col"),) * 5
    return jax.shard_map(
        per_device, mesh=mesh, in_specs=in_specs, out_specs=(P("row", "col"),) * 3, check_vma=False
    )
```

```python
import functools

import jax
import jax.numpy as jnp
from jax import lax
from jax.experimental import pallas as pl
from jax.experimental.pallas import tpu as pltpu
from jax.sharding import PartitionSpec as P

VMEM_BYTES = 24 * 2**20
UPDATE_BYTES = 32 * 2**20
UPDATE_TILE, LAST_TILE = 1024, 256
COST = pl.CostEstimate(flops=1024, bytes_accessed=1024, transcendentals=0)
INNER = 8
CORE, ACROSS, UP = 1, 2, 4
FIRST, SECOND = 0, 1
ONE, OTHER = (ACROSS, UP), (UP, ACROSS)


def beyond(masks):
    return masks[1] | CORE, masks[0] | CORE


BOTH = (ACROSS | UP, ACROSS | UP)
GROUPS = tuple(
    tuple((panel, masks) for who in block for masks in (who, beyond(who)) for panel in (FIRST, SECOND))
    for block in (((0, 0), ONE, OTHER), (BOTH,))
)


def split(value):
    high = value.astype(jnp.bfloat16)
    return high, (value - high.astype(jnp.float32)).astype(jnp.bfloat16)


def product(left, right, contract=1):
    def one(a, b):
        return lax.dot_general(
            a, b, (((contract,), (0,)), ((), ())), preferred_element_type=jnp.float32
        )

    return one(left[0], right[0]) + one(left[0], right[1]) + one(left[1], right[0])


def pack_kernel(*refs):
    (*matrices, first, second), out = refs[:-1], refs[-1]
    rows, width = first.shape
    even = lax.rem(lax.axis_index("col"), 2) == 0
    for k, ref in enumerate(matrices):
        out[k * rows : (k + 1) * rows, :] = jnp.where(even, ref[:, :width], ref[:, width:])
    out[3 * rows : 4 * rows, :] = first[...]
    out[4 * rows :, :] = second[...]


def pack_rows(own):
    rows, width = own[3].shape
    whole = pl.BlockSpec(memory_space=pltpu.VMEM)
    return pl.pallas_call(
        pack_kernel,
        out_shape=jax.ShapeDtypeStruct((5 * rows, width), jnp.float32),
        in_specs=[whole] * 5,
        out_specs=whole,
        cost_estimate=COST,
    )(*own)


def solve_kernel(steps, block, *refs):
    own, refs = refs[:5], refs[5:]
    pieces, (early, late, *refs) = refs[: steps - 1], refs[steps - 1 :]
    outs, (first_out, second_out, *scratch) = refs[: 2 * len(GROUPS)], refs[2 * len(GROUPS) :]
    matrices, right_first, right_second, solved, current = scratch
    here = lax.axis_index("row")
    lane = lax.axis_index("col")
    even = lax.rem(lane, 2) == 0
    rows, width = own[3].shape[0], matrices.shape[2] // 2

    place = jnp.where(lax.rem(here, 2) == 0, here // 2, steps - (here + 1) // 2)

    def at(step):
        back = lax.rem(place + steps - step, steps)
        source = jnp.where(2 * back < steps, 2 * back, 2 * steps - 1 - 2 * back)
        return pl.ds(pl.multiple_of(source * rows, rows), rows)

    for k in range(3):
        matrices[k, at(0), :] = own[k][...]
    right_first[at(0), :] = own[3][...]
    right_second[at(0), :] = own[4][...]
    for j, piece in enumerate(pieces):
        right_first[at(j + 1), :] = piece[3 * rows : 4 * rows, :]
        right_second[at(j + 1), :] = piece[4 * rows :, :]
        for k in range(3):
            mine = piece[k * rows : (k + 1) * rows, :]
            others, at_row = (early, 3 * j + k) if j < steps - 2 else (late, k)
            other = others[at_row * rows : (at_row + 1) * rows, :]
            matrices[k, at(j + 1), :width] = jnp.where(even, mine, other)
            matrices[k, at(j + 1), width:] = jnp.where(even, other, mine)
    current[...] = right_first[...]

    @pl.loop(0, 3)
    def _(k):
        result = product(split(matrices[k]), split(current[...]))
        solved[k] = result
        current[...] = jnp.where(k == 1, right_second[...] - result, result)

    first_out[...] = solved[0, at(0), :]
    second_out[...] = solved[2, at(0), :]

    inner = lax.rem(lane, INNER)
    outer = solved.shape[1] // (INNER * block)
    for group, (high_out, low_out) in zip(GROUPS, zip(outs[::2], outs[1::2])):
        to = 0
        for part, (mask, odd_mask) in group:
            which = lax.bitwise_xor(inner, jnp.where(even, mask, odd_mask))
            for o in range(outer):
                start = pl.multiple_of((o * INNER + which) * block, block)
                high, low = split(solved[2 * part, pl.ds(start, block), :])
                high_out[to : to + block, :] = high
                low_out[to : to + block, :] = low
                to += block


def solve(steps, block, own, pieces, others):
    rows, width = own[3].shape
    depth = rows * steps
    outs = [
        jax.ShapeDtypeStruct((len(group) * depth // INNER, width), jnp.bfloat16)
        for group in GROUPS
        for _ in range(2)
    ]
    outs += [jax.ShapeDtypeStruct((rows, width), jnp.float32)] * 2
    whole = pl.BlockSpec(memory_space=pltpu.VMEM)
    operands = [*own, *pieces, *others]
    return pl.pallas_call(
        functools.partial(solve_kernel, steps, block),
        out_shape=outs,
        in_specs=[whole] * len(operands),
        out_specs=[whole] * len(outs),
        scratch_shapes=[
            pltpu.VMEM((3, depth, depth), jnp.float32),
            pltpu.VMEM((depth, width), jnp.float32),
            pltpu.VMEM((depth, width), jnp.float32),
            pltpu.VMEM((3, depth, width), jnp.float32),
            pltpu.VMEM((depth, width), jnp.float32),
        ],
        compiler_params=pltpu.CompilerParams(vmem_limit_bytes=VMEM_BYTES),
        cost_estimate=COST,
    )(*operands)


def rows_of(t, tile, first=0):
    if isinstance(t, int):
        return pl.ds(first + t * tile, tile)
    return pl.ds(pl.multiple_of(first + t * tile, tile), tile)


def turned_product(panels, factor, rows):
    high, low = split(jnp.concatenate([ref[:, rows] for ref in panels], axis=0))
    left = jnp.concatenate([high, high, low], axis=0)
    right = jnp.concatenate([factor[0], factor[1], factor[0]], axis=0)
    return lax.dot_general(left, right, (((0,), (0,)), ((), ())), preferred_element_type=jnp.float32)


def update_kernel(near_count, far_count, tile, *refs):
    near, refs = refs[:near_count], refs[near_count:]
    far, refs = refs[:far_count], refs[far_count:]
    near_high, near_low, far_high, far_low, before, after, rest, work, arrived, left = refs
    full, tiles = work.shape[0] // tile, before.shape[0] // tile

    def bring(t, to, first):
        here = before.at[rows_of(t, tile), :]
        return pltpu.make_async_copy(here, to.at[rows_of(t - first, tile), :], arrived.at[t])

    def take(t):
        return pltpu.make_async_copy(work.at[rows_of(t, tile), :], after.at[rows_of(t, tile), :], left.at[t])

    for t in range(tiles):
        bring(t, work if t < full else rest, 0 if t < full else full).start()

    @pl.loop(0, full)
    def _(t):
        rows = rows_of(t, tile)
        total = turned_product(near, (near_high[...], near_low[...]), rows)
        total = total + turned_product(far, (far_high[...], far_low[...]), rows)
        bring(t, work, 0).wait()
        work[rows, :] = work[rows, :] - total
        take(t).start()

    @pl.loop(full, tiles)
    def _(t):
        total = turned_product(near, (near_high[...], near_low[...]), rows_of(t, tile))
        bring(t, rest, full).wait()
        rows = rows_of(t - full, tile)
        rest[rows, :] = rest[rows, :] - total

    for t in range(full):
        take(t).wait()


def update(near, near_factor, far, far_factor, before):
    rows, width, full = before.shape[0], before.shape[1], far[0].shape[1]
    tile = min(UPDATE_TILE, full)
    operands = [*near, *far, *near_factor, *far_factor]
    anywhere, inside = pl.BlockSpec(memory_space=pl.ANY), pl.BlockSpec(memory_space=pltpu.VMEM)
    return pl.pallas_call(
        functools.partial(update_kernel, len(near), len(far), tile),
        out_shape=[
            jax.ShapeDtypeStruct(before.shape, jnp.float32),
            jax.ShapeDtypeStruct((rows - full, width), jnp.float32),
        ],
        in_specs=[inside] * len(operands) + [anywhere],
        out_specs=[anywhere, inside],
        scratch_shapes=[
            pltpu.VMEM((full, width), jnp.float32),
            pltpu.SemaphoreType.DMA((rows // tile,)),
            pltpu.SemaphoreType.DMA((full // tile,)),
        ],
        compiler_params=pltpu.CompilerParams(vmem_limit_bytes=UPDATE_BYTES),
        cost_estimate=COST,
    )(*operands, before)


def subtract_kernel(tile, panel, high, low, before, after):
    @pl.loop(0, before.shape[0] // tile)
    def _(t):
        rows = rows_of(t, tile)
        half = pl.ds(0, panel.shape[0])
        after[rows, :] = before[rows, :] - turned_product([panel], (high[half, :], low[half, :]), rows)


def subtract(panel, factor, before):
    inside = pl.BlockSpec(memory_space=pltpu.VMEM)
    return pl.pallas_call(
        functools.partial(subtract_kernel, min(LAST_TILE, before.shape[0])),
        out_shape=jax.ShapeDtypeStruct(before.shape, jnp.float32),
        in_specs=[inside] * 4,
        out_specs=inside,
        input_output_aliases={3: 0},
        compiler_params=pltpu.CompilerParams(vmem_limit_bytes=VMEM_BYTES),
        cost_estimate=COST,
    )(panel, *factor, before)


def finish_kernel(tile, panel, high, low, rest, before, after, work, left):
    rows, start = rest.shape[0], after.shape[0] - rest.shape[0]

    def take(t):
        to = after.at[rows_of(t, tile, start), :]
        return pltpu.make_async_copy(work.at[rows_of(t, tile), :], to, left.at[t])

    for t in range(rows // tile):
        here = rows_of(t, tile)
        half = pl.ds(panel.shape[0], panel.shape[0])
        work[here, :] = rest[here, :] - turned_product([panel], (high[half, :], low[half, :]), here)
        take(t).start()
    for t in range(rows // tile):
        take(t).wait()


def finish(panel, factor, rest, before):
    rows = rest.shape[0]
    tile = min(LAST_TILE, rows)
    anywhere, inside = pl.BlockSpec(memory_space=pl.ANY), pl.BlockSpec(memory_space=pltpu.VMEM)
    return pl.pallas_call(
        functools.partial(finish_kernel, tile),
        out_shape=jax.ShapeDtypeStruct(before.shape, jnp.float32),
        in_specs=[inside] * 4 + [anywhere],
        out_specs=anywhere,
        input_output_aliases={4: 0},
        scratch_shapes=[pltpu.VMEM(rest.shape, jnp.float32), pltpu.SemaphoreType.DMA((rows // tile,))],
        compiler_params=pltpu.CompilerParams(vmem_limit_bytes=VMEM_BYTES),
        cost_estimate=COST,
    )(panel, *factor, rest, before)


def solution(mesh):
    row_count, col_count = mesh.shape["row"], mesh.shape["col"]

    def swap(value, bit):
        return lax.ppermute(value, "col", [(i, i ^ bit) for i in range(col_count)])

    ring = [*range(0, row_count, 2), *reversed(range(1, row_count, 2))]

    def onward(value):
        return lax.ppermute(value, "row", list(zip(ring, ring[1:] + ring[:1])))

    def per_device(
        inverse_first, inverse_second, coupling, panel_first, panel_second,
        rhs_first, rhs_second, rhs_rest,
    ):
        first, second = panel_first.T, panel_second.T
        block = first.shape[0]
        if col_count > INNER:
            groups = [list(range(i, col_count, INNER)) for i in range(INNER)]
            first, second = (
                lax.all_gather(p, "col", axis=0, tiled=True, axis_index_groups=groups)
                for p in (first, second)
            )
        rest = first.shape[1]

        own = (inverse_first, coupling, inverse_second, rhs_first, rhs_second)
        def cross(value, masks):
            return lax.ppermute(value, "col", [(i, i ^ masks[i % 2]) for i in range(col_count)])

        def beside(pair):
            return tuple(swap(x, CORE) for x in pair)

        def halves(value):
            return jnp.split(value, 2, axis=0)

        def after(values, *tokens):
            return lax.optimization_barrier((values, tokens))[0]

        near_0 = tuple(cross(x, ONE) for x in (first, second))
        own_beside = beside((first, second))
        matrix_rows = 3 * rhs_first.shape[0]
        packs = [onward(pack_rows(own))]
        near_1 = tuple(cross(x, OTHER) for x in after((first, second), own_beside, packs[0]))
        beside_0 = beside(near_0)
        for j in range(row_count - 2):
            packs.append(onward(after(packs[-1], beside_0[0]) if j == row_count - 3 else packs[-1]))
        beside_1 = beside(halves(near_1[0]))
        cuts = [0, rest // 2, rest]

        def far_part(pair, a, b):
            return cross(jnp.concatenate([x[:, a:b] for x in pair], axis=0), OTHER)

        far = [far_part(near_0, cuts[0], cuts[1])]
        early = swap(jnp.concatenate([p[:matrix_rows] for p in packs[:-1]], axis=0), CORE)
        near_0, near_1, beside_0, beside_1, packs, early = lax.optimization_barrier(
            (near_0, near_1, beside_0, beside_1, packs, early)
        )
        far += [far_part(near_0, a, b) for a, b in zip(cuts[1:-1], cuts[2:])]
        others = early, swap(packs[-1][:matrix_rows], CORE)
        beside_1 += beside(halves(after(near_1[1], others)))
        near = [
            panel
            for pair in ((first, second), own_beside, near_0, beside_0, near_1, beside_1)
            for panel in pair
        ]
        *factors, solved_first, solved_second = solve(row_count, block, own, packs, others)
        near_factor, far_factor = factors[:2], factors[2:]
        near_far = [far[0], *beside(halves(after(far[0], others)))]
        updated, last = update(near, near_factor, near_far, far_factor, rhs_rest)
        panel = after(far[1], updated)
        other = swap(panel, CORE)
        updated = finish(other, far_factor, subtract(panel, far_factor, last), updated)
        return solved_first, solved_second, updated

    in_specs = (P("row", None),) * 3 + (P("row", "col"),) * 5
    return jax.shard_map(
        per_device, mesh=mesh, in_specs=in_specs, out_specs=(P("row", "col"),) * 3, check_vma=False
    )
```

```python
import functools

import jax
import jax.numpy as jnp
from jax import lax
from jax.experimental import pallas as pl
from jax.experimental.pallas import tpu as pltpu
from jax.sharding import PartitionSpec as P

VMEM_BYTES = 24 * 2**20
UPDATE_BYTES = 32 * 2**20
UPDATE_TILE, LAST_TILE = 1024, 256
COST = pl.CostEstimate(flops=1024, bytes_accessed=1024, transcendentals=0)
INNER = 8
CORE, ACROSS, UP = 1, 2, 4
FIRST, SECOND = 0, 1
ONE, OTHER = (ACROSS, UP), (UP, ACROSS)


def beyond(masks):
    return masks[1] | CORE, masks[0] | CORE


BOTH = (ACROSS | UP, ACROSS | UP)
GROUPS = tuple(
    tuple((panel, masks) for who in block for masks in (who, beyond(who)) for panel in (FIRST, SECOND))
    for block in (((0, 0), ONE, OTHER), (BOTH,))
)


def split(value):
    high = value.astype(jnp.bfloat16)
    return high, (value - high.astype(jnp.float32)).astype(jnp.bfloat16)


def product(left, right, contract=1):
    def one(a, b):
        return lax.dot_general(
            a, b, (((contract,), (0,)), ((), ())), preferred_element_type=jnp.float32
        )

    return one(left[0], right[0]) + one(left[0], right[1]) + one(left[1], right[0])


def pack_kernel(*refs):
    (*matrices, first, second), out = refs[:-1], refs[-1]
    rows, width = first.shape
    even = lax.rem(lax.axis_index("col"), 2) == 0
    for k, ref in enumerate(matrices):
        out[k * rows : (k + 1) * rows, :] = jnp.where(even, ref[:, :width], ref[:, width:])
    out[3 * rows : 4 * rows, :] = first[...]
    out[4 * rows :, :] = second[...]


def pack_rows(own):
    rows, width = own[3].shape
    whole = pl.BlockSpec(memory_space=pltpu.VMEM)
    return pl.pallas_call(
        pack_kernel,
        out_shape=jax.ShapeDtypeStruct((5 * rows, width), jnp.float32),
        in_specs=[whole] * 5,
        out_specs=whole,
        cost_estimate=COST,
    )(*own)


def solve_kernel(steps, block, *refs):
    own, refs = refs[:5], refs[5:]
    pieces, (early, late, *refs) = refs[: steps - 1], refs[steps - 1 :]
    outs, (first_out, second_out, *scratch) = refs[: 2 * len(GROUPS)], refs[2 * len(GROUPS) :]
    matrices, right_first, right_second, solved, current = scratch
    here = lax.axis_index("row")
    lane = lax.axis_index("col")
    even = lax.rem(lane, 2) == 0
    rows, width = own[3].shape[0], matrices.shape[2] // 2

    place = jnp.where(lax.rem(here, 2) == 0, here // 2, steps - (here + 1) // 2)

    def at(step):
        back = lax.rem(place + steps - step, steps)
        source = jnp.where(2 * back < steps, 2 * back, 2 * steps - 1 - 2 * back)
        return pl.ds(pl.multiple_of(source * rows, rows), rows)

    for k in range(3):
        matrices[k, at(0), :] = own[k][...]
    right_first[at(0), :] = own[3][...]
    right_second[at(0), :] = own[4][...]
    for j, piece in enumerate(pieces):
        right_first[at(j + 1), :] = piece[3 * rows : 4 * rows, :]
        right_second[at(j + 1), :] = piece[4 * rows :, :]
        for k in range(3):
            mine = piece[k * rows : (k + 1) * rows, :]
            others, at_row = (early, 3 * j + k) if j < steps - 2 else (late, k)
            other = others[at_row * rows : (at_row + 1) * rows, :]
            matrices[k, at(j + 1), :width] = jnp.where(even, mine, other)
            matrices[k, at(j + 1), width:] = jnp.where(even, other, mine)
    current[...] = right_first[...]

    @pl.loop(0, 3)
    def _(k):
        result = product(split(matrices[k]), split(current[...]))
        solved[k] = result
        current[...] = jnp.where(k == 1, right_second[...] - result, result)

    first_out[...] = solved[0, at(0), :]
    second_out[...] = solved[2, at(0), :]

    inner = lax.rem(lane, INNER)
    outer = solved.shape[1] // (INNER * block)
    for group, (high_out, low_out) in zip(GROUPS, zip(outs[::2], outs[1::2])):
        to = 0
        for part, (mask, odd_mask) in group:
            which = lax.bitwise_xor(inner, jnp.where(even, mask, odd_mask))
            for o in range(outer):
                start = pl.multiple_of((o * INNER + which) * block, block)
                high, low = split(solved[2 * part, pl.ds(start, block), :])
                high_out[to : to + block, :] = high
                low_out[to : to + block, :] = low
                to += block


def solve(steps, block, own, pieces, others):
    rows, width = own[3].shape
    depth = rows * steps
    outs = [
        jax.ShapeDtypeStruct((len(group) * depth // INNER, width), jnp.bfloat16)
        for group in GROUPS
        for _ in range(2)
    ]
    outs += [jax.ShapeDtypeStruct((rows, width), jnp.float32)] * 2
    whole = pl.BlockSpec(memory_space=pltpu.VMEM)
    operands = [*own, *pieces, *others]
    return pl.pallas_call(
        functools.partial(solve_kernel, steps, block),
        out_shape=outs,
        in_specs=[whole] * len(operands),
        out_specs=[whole] * len(outs),
        scratch_shapes=[
            pltpu.VMEM((3, depth, depth), jnp.float32),
            pltpu.VMEM((depth, width), jnp.float32),
            pltpu.VMEM((depth, width), jnp.float32),
            pltpu.VMEM((3, depth, width), jnp.float32),
            pltpu.VMEM((depth, width), jnp.float32),
        ],
        compiler_params=pltpu.CompilerParams(vmem_limit_bytes=VMEM_BYTES),
        cost_estimate=COST,
    )(*operands)


def rows_of(t, tile, first=0):
    if isinstance(t, int):
        return pl.ds(first + t * tile, tile)
    return pl.ds(pl.multiple_of(first + t * tile, tile), tile)


def turned_product(panels, factor, rows):
    high, low = split(jnp.concatenate([ref[:, rows] for ref in panels], axis=0))
    left = jnp.concatenate([high, high, low], axis=0)
    right = jnp.concatenate([factor[0], factor[1], factor[0]], axis=0)
    return lax.dot_general(left, right, (((0,), (0,)), ((), ())), preferred_element_type=jnp.float32)


def update_kernel(near_count, far_count, tile, *refs):
    near, refs = refs[:near_count], refs[near_count:]
    far, refs = refs[:far_count], refs[far_count:]
    near_high, near_low, far_high, far_low, before, after, rest, work, arrived, left = refs
    full, tiles = work.shape[0] // tile, before.shape[0] // tile

    def bring(t, to, first):
        here = before.at[rows_of(t, tile), :]
        return pltpu.make_async_copy(here, to.at[rows_of(t - first, tile), :], arrived.at[t])

    def take(t):
        return pltpu.make_async_copy(work.at[rows_of(t, tile), :], after.at[rows_of(t, tile), :], left.at[t])

    for t in range(tiles):
        bring(t, work if t < full else rest, 0 if t < full else full).start()

    @pl.loop(0, full)
    def _(t):
        rows = rows_of(t, tile)
        total = turned_product(near, (near_high[...], near_low[...]), rows)
        total = total + turned_product(far, (far_high[...], far_low[...]), rows)
        bring(t, work, 0).wait()
        work[rows, :] = work[rows, :] - total
        take(t).start()

    @pl.loop(full, tiles)
    def _(t):
        total = turned_product(near, (near_high[...], near_low[...]), rows_of(t, tile))
        bring(t, rest, full).wait()
        rows = rows_of(t - full, tile)
        rest[rows, :] = rest[rows, :] - total

    for t in range(full):
        take(t).wait()


def update(near, near_factor, far, far_factor, before):
    rows, width, full = before.shape[0], before.shape[1], far[0].shape[1]
    tile = min(UPDATE_TILE, full)
    operands = [*near, *far, *near_factor, *far_factor]
    anywhere, inside = pl.BlockSpec(memory_space=pl.ANY), pl.BlockSpec(memory_space=pltpu.VMEM)
    return pl.pallas_call(
        functools.partial(update_kernel, len(near), len(far), tile),
        out_shape=[
            jax.ShapeDtypeStruct(before.shape, jnp.float32),
            jax.ShapeDtypeStruct((rows - full, width), jnp.float32),
        ],
        in_specs=[inside] * len(operands) + [anywhere],
        out_specs=[anywhere, inside],
        scratch_shapes=[
            pltpu.VMEM((full, width), jnp.float32),
            pltpu.SemaphoreType.DMA((rows // tile,)),
            pltpu.SemaphoreType.DMA((full // tile,)),
        ],
        compiler_params=pltpu.CompilerParams(vmem_limit_bytes=UPDATE_BYTES),
        cost_estimate=COST,
    )(*operands, before)


def subtract_kernel(tile, panel, high, low, before, after):
    @pl.loop(0, before.shape[0] // tile)
    def _(t):
        rows = rows_of(t, tile)
        half = pl.ds(0, panel.shape[0])
        after[rows, :] = before[rows, :] - turned_product([panel], (high[half, :], low[half, :]), rows)


def subtract(panel, factor, before):
    inside = pl.BlockSpec(memory_space=pltpu.VMEM)
    return pl.pallas_call(
        functools.partial(subtract_kernel, min(UPDATE_TILE, before.shape[0])),
        out_shape=jax.ShapeDtypeStruct(before.shape, jnp.float32),
        in_specs=[inside] * 4,
        out_specs=inside,
        input_output_aliases={3: 0},
        compiler_params=pltpu.CompilerParams(vmem_limit_bytes=VMEM_BYTES),
        cost_estimate=COST,
    )(panel, *factor, before)


def finish_kernel(tile, panel, high, low, rest, before, after, work, left):
    rows, start = rest.shape[0], after.shape[0] - rest.shape[0]

    def take(t):
        to = after.at[rows_of(t, tile, start), :]
        return pltpu.make_async_copy(work.at[rows_of(t, tile), :], to, left.at[t])

    for t in range(rows // tile):
        here = rows_of(t, tile)
        half = pl.ds(panel.shape[0], panel.shape[0])
        work[here, :] = rest[here, :] - turned_product([panel], (high[half, :], low[half, :]), here)
        take(t).start()
    for t in range(rows // tile):
        take(t).wait()


def finish(panel, factor, rest, before):
    rows = rest.shape[0]
    tile = min(LAST_TILE, rows)
    anywhere, inside = pl.BlockSpec(memory_space=pl.ANY), pl.BlockSpec(memory_space=pltpu.VMEM)
    return pl.pallas_call(
        functools.partial(finish_kernel, tile),
        out_shape=jax.ShapeDtypeStruct(before.shape, jnp.float32),
        in_specs=[inside] * 4 + [anywhere],
        out_specs=anywhere,
        input_output_aliases={4: 0},
        scratch_shapes=[pltpu.VMEM(rest.shape, jnp.float32), pltpu.SemaphoreType.DMA((rows // tile,))],
        compiler_params=pltpu.CompilerParams(vmem_limit_bytes=VMEM_BYTES),
        cost_estimate=COST,
    )(panel, *factor, rest, before)


def solution(mesh):
    row_count, col_count = mesh.shape["row"], mesh.shape["col"]

    def swap(value, bit):
        return lax.ppermute(value, "col", [(i, i ^ bit) for i in range(col_count)])

    ring = [*range(0, row_count, 2), *reversed(range(1, row_count, 2))]

    def onward(value):
        return lax.ppermute(value, "row", list(zip(ring, ring[1:] + ring[:1])))

    def per_device(
        inverse_first, inverse_second, coupling, panel_first, panel_second,
        rhs_first, rhs_second, rhs_rest,
    ):
        first, second = panel_first.T, panel_second.T
        block = first.shape[0]
        if col_count > INNER:
            groups = [list(range(i, col_count, INNER)) for i in range(INNER)]
            first, second = (
                lax.all_gather(p, "col", axis=0, tiled=True, axis_index_groups=groups)
                for p in (first, second)
            )
        rest = first.shape[1]

        own = (inverse_first, coupling, inverse_second, rhs_first, rhs_second)
        def cross(value, masks):
            return lax.ppermute(value, "col", [(i, i ^ masks[i % 2]) for i in range(col_count)])

        def beside(pair):
            return tuple(swap(x, CORE) for x in pair)

        def halves(value):
            return jnp.split(value, 2, axis=0)

        def after(values, *tokens):
            return lax.optimization_barrier((values, tokens))[0]

        near_0 = tuple(cross(x, ONE) for x in (first, second))
        own_beside = beside((first, second))
        matrix_rows = 3 * rhs_first.shape[0]
        packs = [onward(pack_rows(own))]
        near_1 = tuple(cross(x, OTHER) for x in after((first, second), own_beside, packs[0]))
        beside_0 = beside(near_0)
        for j in range(row_count - 2):
            packs.append(onward(after(packs[-1], beside_0[0]) if j == row_count - 3 else packs[-1]))
        beside_1 = beside(halves(near_1[0]))
        cuts = [0, rest // 2, rest]

        def far_part(pair, a, b):
            return cross(jnp.concatenate([x[:, a:b] for x in pair], axis=0), OTHER)

        far = [far_part(near_0, cuts[0], cuts[1])]
        early = swap(jnp.concatenate([p[:matrix_rows] for p in packs[:-1]], axis=0), CORE)
        near_0, near_1, beside_0, beside_1, packs, early = lax.optimization_barrier(
            (near_0, near_1, beside_0, beside_1, packs, early)
        )
        far += [far_part(near_0, a, b) for a, b in zip(cuts[1:-1], cuts[2:])]
        others = early, swap(packs[-1][:matrix_rows], CORE)
        beside_1 += beside(halves(after(near_1[1], others)))
        near = [
            panel
            for pair in ((first, second), own_beside, near_0, beside_0, near_1, beside_1)
            for panel in pair
        ]
        *factors, solved_first, solved_second = solve(row_count, block, own, packs, others)
        near_factor, far_factor = factors[:2], factors[2:]
        near_far = [far[0], *beside(halves(after(far[0], others)))]
        updated, last = update(near, near_factor, near_far, far_factor, rhs_rest)
        panel = after(far[1], updated)
        other = swap(panel, CORE)
        updated = finish(other, far_factor, subtract(panel, far_factor, last), updated)
        return solved_first, solved_second, updated

    in_specs = (P("row", None),) * 3 + (P("row", "col"),) * 5
    return jax.shard_map(
        per_device, mesh=mesh, in_specs=in_specs, out_specs=(P("row", "col"),) * 3, check_vma=False
    )
```

```python
import functools

import jax
import jax.numpy as jnp
from jax import lax
from jax.experimental import pallas as pl
from jax.experimental.pallas import tpu as pltpu
from jax.sharding import PartitionSpec as P

VMEM_BYTES = 24 * 2**20
UPDATE_BYTES = 32 * 2**20
UPDATE_TILE, LAST_TILE = 1024, 256
COST = pl.CostEstimate(flops=1024, bytes_accessed=1024, transcendentals=0)
INNER = 8
CORE, ACROSS, UP = 1, 2, 4
FIRST, SECOND = 0, 1
ONE, OTHER = (UP, ACROSS), (ACROSS, UP)


def beyond(masks):
    return masks[1] | CORE, masks[0] | CORE


BOTH = (ACROSS | UP, ACROSS | UP)
GROUPS = tuple(
    tuple((panel, masks) for who in block for masks in (who, beyond(who)) for panel in (FIRST, SECOND))
    for block in (((0, 0), ONE, OTHER), (BOTH,))
)


def split(value):
    high = value.astype(jnp.bfloat16)
    return high, (value - high.astype(jnp.float32)).astype(jnp.bfloat16)


def product(left, right, contract=1):
    def one(a, b):
        return lax.dot_general(
            a, b, (((contract,), (0,)), ((), ())), preferred_element_type=jnp.float32
        )

    return one(left[0], right[0]) + one(left[0], right[1]) + one(left[1], right[0])


def pack_kernel(*refs):
    (*matrices, first, second), out = refs[:-1], refs[-1]
    rows, width = first.shape
    even = lax.rem(lax.axis_index("col"), 2) == 0
    for k, ref in enumerate(matrices):
        out[k * rows : (k + 1) * rows, :] = jnp.where(even, ref[:, :width], ref[:, width:])
    out[3 * rows : 4 * rows, :] = first[...]
    out[4 * rows :, :] = second[...]


def pack_rows(own):
    rows, width = own[3].shape
    whole = pl.BlockSpec(memory_space=pltpu.VMEM)
    return pl.pallas_call(
        pack_kernel,
        out_shape=jax.ShapeDtypeStruct((5 * rows, width), jnp.float32),
        in_specs=[whole] * 5,
        out_specs=whole,
        cost_estimate=COST,
    )(*own)


def solve_kernel(steps, block, *refs):
    own, refs = refs[:5], refs[5:]
    pieces, (early, late, *refs) = refs[: steps - 1], refs[steps - 1 :]
    outs, (first_out, second_out, *scratch) = refs[: 2 * len(GROUPS)], refs[2 * len(GROUPS) :]
    matrices, right_first, right_second, solved, current = scratch
    here = lax.axis_index("row")
    lane = lax.axis_index("col")
    even = lax.rem(lane, 2) == 0
    rows, width = own[3].shape[0], matrices.shape[2] // 2

    place = jnp.where(lax.rem(here, 2) == 0, here // 2, steps - (here + 1) // 2)

    def at(step):
        back = lax.rem(place + steps - step, steps)
        source = jnp.where(2 * back < steps, 2 * back, 2 * steps - 1 - 2 * back)
        return pl.ds(pl.multiple_of(source * rows, rows), rows)

    for k in range(3):
        matrices[k, at(0), :] = own[k][...]
    right_first[at(0), :] = own[3][...]
    right_second[at(0), :] = own[4][...]
    for j, piece in enumerate(pieces):
        right_first[at(j + 1), :] = piece[3 * rows : 4 * rows, :]
        right_second[at(j + 1), :] = piece[4 * rows :, :]
        for k in range(3):
            mine = piece[k * rows : (k + 1) * rows, :]
            others, at_row = (early, 3 * j + k) if j < steps - 2 else (late, k)
            other = others[at_row * rows : (at_row + 1) * rows, :]
            matrices[k, at(j + 1), :width] = jnp.where(even, mine, other)
            matrices[k, at(j + 1), width:] = jnp.where(even, other, mine)
    current[...] = right_first[...]

    @pl.loop(0, 3)
    def _(k):
        result = product(split(matrices[k]), split(current[...]))
        solved[k] = result
        current[...] = jnp.where(k == 1, right_second[...] - result, result)

    first_out[...] = solved[0, at(0), :]
    second_out[...] = solved[2, at(0), :]

    inner = lax.rem(lane, INNER)
    outer = solved.shape[1] // (INNER * block)
    for group, (high_out, low_out) in zip(GROUPS, zip(outs[::2], outs[1::2])):
        to = 0
        for part, (mask, odd_mask) in group:
            which = lax.bitwise_xor(inner, jnp.where(even, mask, odd_mask))
            for o in range(outer):
                start = pl.multiple_of((o * INNER + which) * block, block)
                high, low = split(solved[2 * part, pl.ds(start, block), :])
                high_out[to : to + block, :] = high
                low_out[to : to + block, :] = low
                to += block


def solve(steps, block, own, pieces, others):
    rows, width = own[3].shape
    depth = rows * steps
    outs = [
        jax.ShapeDtypeStruct((len(group) * depth // INNER, width), jnp.bfloat16)
        for group in GROUPS
        for _ in range(2)
    ]
    outs += [jax.ShapeDtypeStruct((rows, width), jnp.float32)] * 2
    whole = pl.BlockSpec(memory_space=pltpu.VMEM)
    operands = [*own, *pieces, *others]
    return pl.pallas_call(
        functools.partial(solve_kernel, steps, block),
        out_shape=outs,
        in_specs=[whole] * len(operands),
        out_specs=[whole] * len(outs),
        scratch_shapes=[
            pltpu.VMEM((3, depth, depth), jnp.float32),
            pltpu.VMEM((depth, width), jnp.float32),
            pltpu.VMEM((depth, width), jnp.float32),
            pltpu.VMEM((3, depth, width), jnp.float32),
            pltpu.VMEM((depth, width), jnp.float32),
        ],
        compiler_params=pltpu.CompilerParams(vmem_limit_bytes=VMEM_BYTES),
        cost_estimate=COST,
    )(*operands)


def rows_of(t, tile, first=0):
    if isinstance(t, int):
        return pl.ds(first + t * tile, tile)
    return pl.ds(pl.multiple_of(first + t * tile, tile), tile)


def turned_product(panels, factor, rows):
    high, low = split(jnp.concatenate([ref[:, rows] for ref in panels], axis=0))
    left = jnp.concatenate([high, high, low], axis=0)
    right = jnp.concatenate([factor[0], factor[1], factor[0]], axis=0)
    return lax.dot_general(left, right, (((0,), (0,)), ((), ())), preferred_element_type=jnp.float32)


def update_kernel(near_count, far_count, tile, *refs):
    near, refs = refs[:near_count], refs[near_count:]
    far, refs = refs[:far_count], refs[far_count:]
    near_high, near_low, far_high, far_low, before, after, rest, work, arrived, left = refs
    full, tiles = work.shape[0] // tile, before.shape[0] // tile

    def bring(t, to, first):
        here = before.at[rows_of(t, tile), :]
        return pltpu.make_async_copy(here, to.at[rows_of(t - first, tile), :], arrived.at[t])

    def take(t):
        return pltpu.make_async_copy(work.at[rows_of(t, tile), :], after.at[rows_of(t, tile), :], left.at[t])

    for t in range(tiles):
        bring(t, work if t < full else rest, 0 if t < full else full).start()

    @pl.loop(0, full)
    def _(t):
        rows = rows_of(t, tile)
        total = turned_product(near, (near_high[...], near_low[...]), rows)
        total = total + turned_product(far, (far_high[...], far_low[...]), rows)
        bring(t, work, 0).wait()
        work[rows, :] = work[rows, :] - total
        take(t).start()

    @pl.loop(full, tiles)
    def _(t):
        total = turned_product(near, (near_high[...], near_low[...]), rows_of(t, tile))
        bring(t, rest, full).wait()
        rows = rows_of(t - full, tile)
        rest[rows, :] = rest[rows, :] - total

    for t in range(full):
        take(t).wait()


def update(near, near_factor, far, far_factor, before):
    rows, width, full = before.shape[0], before.shape[1], far[0].shape[1]
    tile = min(UPDATE_TILE, full)
    operands = [*near, *far, *near_factor, *far_factor]
    anywhere, inside = pl.BlockSpec(memory_space=pl.ANY), pl.BlockSpec(memory_space=pltpu.VMEM)
    return pl.pallas_call(
        functools.partial(update_kernel, len(near), len(far), tile),
        out_shape=[
            jax.ShapeDtypeStruct(before.shape, jnp.float32),
            jax.ShapeDtypeStruct((rows - full, width), jnp.float32),
        ],
        in_specs=[inside] * len(operands) + [anywhere],
        out_specs=[anywhere, inside],
        scratch_shapes=[
            pltpu.VMEM((full, width), jnp.float32),
            pltpu.SemaphoreType.DMA((rows // tile,)),
            pltpu.SemaphoreType.DMA((full // tile,)),
        ],
        compiler_params=pltpu.CompilerParams(vmem_limit_bytes=UPDATE_BYTES),
        cost_estimate=COST,
    )(*operands, before)


def subtract_kernel(tile, panel, high, low, before, after):
    @pl.loop(0, before.shape[0] // tile)
    def _(t):
        rows = rows_of(t, tile)
        half = pl.ds(0, panel.shape[0])
        after[rows, :] = before[rows, :] - turned_product([panel], (high[half, :], low[half, :]), rows)


def subtract(panel, factor, before):
    inside = pl.BlockSpec(memory_space=pltpu.VMEM)
    return pl.pallas_call(
        functools.partial(subtract_kernel, min(UPDATE_TILE, before.shape[0])),
        out_shape=jax.ShapeDtypeStruct(before.shape, jnp.float32),
        in_specs=[inside] * 4,
        out_specs=inside,
        input_output_aliases={3: 0},
        compiler_params=pltpu.CompilerParams(vmem_limit_bytes=VMEM_BYTES),
        cost_estimate=COST,
    )(panel, *factor, before)


def finish_kernel(tile, panel, high, low, rest, before, after, work, left):
    rows, start = rest.shape[0], after.shape[0] - rest.shape[0]

    def take(t):
        to = after.at[rows_of(t, tile, start), :]
        return pltpu.make_async_copy(work.at[rows_of(t, tile), :], to, left.at[t])

    for t in range(rows // tile):
        here = rows_of(t, tile)
        half = pl.ds(panel.shape[0], panel.shape[0])
        work[here, :] = rest[here, :] - turned_product([panel], (high[half, :], low[half, :]), here)
        take(t).start()
    for t in range(rows // tile):
        take(t).wait()


def finish(panel, factor, rest, before):
    rows = rest.shape[0]
    tile = min(LAST_TILE, rows)
    anywhere, inside = pl.BlockSpec(memory_space=pl.ANY), pl.BlockSpec(memory_space=pltpu.VMEM)
    return pl.pallas_call(
        functools.partial(finish_kernel, tile),
        out_shape=jax.ShapeDtypeStruct(before.shape, jnp.float32),
        in_specs=[inside] * 4 + [anywhere],
        out_specs=anywhere,
        input_output_aliases={4: 0},
        scratch_shapes=[pltpu.VMEM(rest.shape, jnp.float32), pltpu.SemaphoreType.DMA((rows // tile,))],
        compiler_params=pltpu.CompilerParams(vmem_limit_bytes=VMEM_BYTES),
        cost_estimate=COST,
    )(panel, *factor, rest, before)


def solution(mesh):
    row_count, col_count = mesh.shape["row"], mesh.shape["col"]

    def swap(value, bit):
        return lax.ppermute(value, "col", [(i, i ^ bit) for i in range(col_count)])

    ring = [*range(0, row_count, 2), *reversed(range(1, row_count, 2))]

    def onward(value):
        return lax.ppermute(value, "row", list(zip(ring, ring[1:] + ring[:1])))

    def per_device(
        inverse_first, inverse_second, coupling, panel_first, panel_second,
        rhs_first, rhs_second, rhs_rest,
    ):
        first, second = panel_first.T, panel_second.T
        block = first.shape[0]
        if col_count > INNER:
            groups = [list(range(i, col_count, INNER)) for i in range(INNER)]
            first, second = (
                lax.all_gather(p, "col", axis=0, tiled=True, axis_index_groups=groups)
                for p in (first, second)
            )
        rest = first.shape[1]

        own = (inverse_first, coupling, inverse_second, rhs_first, rhs_second)
        def cross(value, masks):
            return lax.ppermute(value, "col", [(i, i ^ masks[i % 2]) for i in range(col_count)])

        def beside(pair):
            return tuple(swap(x, CORE) for x in pair)

        def halves(value):
            return jnp.split(value, 2, axis=0)

        def after(values, *tokens):
            return lax.optimization_barrier((values, tokens))[0]

        near_0 = tuple(cross(x, ONE) for x in (first, second))
        own_beside = beside((first, second))
        matrix_rows = 3 * rhs_first.shape[0]
        packs = [onward(pack_rows(own))]
        near_1 = tuple(cross(x, OTHER) for x in after((first, second), own_beside, packs[0]))
        beside_0 = beside(near_0)
        for j in range(row_count - 2):
            packs.append(onward(after(packs[-1], beside_0[0]) if j == row_count - 3 else packs[-1]))
        beside_1 = beside(halves(near_1[0]))
        cuts = [0, rest // 2, rest]

        def far_part(pair, a, b):
            return cross(jnp.concatenate([x[:, a:b] for x in pair], axis=0), OTHER)

        far = [far_part(near_0, cuts[0], cuts[1])]
        early = swap(jnp.concatenate([p[:matrix_rows] for p in packs[:-1]], axis=0), CORE)
        near_0, near_1, beside_0, beside_1, packs, early = lax.optimization_barrier(
            (near_0, near_1, beside_0, beside_1, packs, early)
        )
        far += [far_part(near_0, a, b) for a, b in zip(cuts[1:-1], cuts[2:])]
        others = early, swap(packs[-1][:matrix_rows], CORE)
        beside_1 += beside(halves(after(near_1[1], others)))
        near = [
            panel
            for pair in ((first, second), own_beside, near_0, beside_0, near_1, beside_1)
            for panel in pair
        ]
        *factors, solved_first, solved_second = solve(row_count, block, own, packs, others)
        near_factor, far_factor = factors[:2], factors[2:]
        near_far = [far[0], *beside(halves(after(far[0], others)))]
        updated, last = update(near, near_factor, near_far, far_factor, rhs_rest)
        panel = after(far[1], updated)
        other = swap(panel, CORE)
        updated = finish(other, far_factor, subtract(panel, far_factor, last), updated)
        return solved_first, solved_second, updated

    in_specs = (P("row", None),) * 3 + (P("row", "col"),) * 5
    return jax.shard_map(
        per_device, mesh=mesh, in_specs=in_specs, out_specs=(P("row", "col"),) * 3, check_vma=False
    )
```
